128 devices in a mesh: gx: 16 (over x, z_hi, core), gy: 8 (over y, z_lo).
Axes of the slice: x: 4, y: 4, z: 4 (z_hi: 2, z_lo: 2; z = z_hi * 2 + z_lo), core: 2. Of those that a mesh axis runs over, the one named last changes fastest.
Arguments:
- fields: float32 [4, 3, 64, 16, 16, 128], P(None, None, None, 'gx', 'gy'), may hold values from -6 to 6
- velocity: float32 [2, 3, 64, 128, 16, 16], P(None, None, None, ('gx', 'gy')), may hold values from -3 to 3
Outputs:
- advanced: float32 [4, 3, 64, 16, 16, 128], P(None, None, None, 'gx', 'gy')
The draws below stay inside these ranges and needn't reach their ends.
All inputs are finite; a program needn't handle non-finite values.
Results may differ from the reference program's by a relative error of at most 0.0003.
Values sent between devices are 32-bit elements; how exact they have to be, the bound alone decides.
No kernel may reach another device: no remote copies, remote signals or barrier semaphores. Data moves between devices by JAX's collectives and lax.ppermute only.
A program may use at most 64 MiB of HBM per device.

```python
import jax
import jax.numpy as jnp
import numpy as np
from jax import lax

K = 4
NODES = 64
EZ = 128
STEPS = 2
NXE = 16
NYE = 16


def shard_levels(own_key, shape, split, least, top_value):
    def one(dim, blocks):
        draws = jax.random.uniform(jax.random.fold_in(jax.random.fold_in(own_key, 6), dim), (blocks,), jnp.float32, least / len(split), top_value / len(split))
        return jnp.repeat(jnp.exp(draws), shape[dim] // blocks).reshape((-1,) + (1,) * (len(shape) - dim - 1))

    factor_of = one(*split[0])
    for cut in split[1:]:
        factor_of = factor_of * one(*cut)
    return factor_of


def centred(rng, shape, deviation, bound, shards=(), dtype=jnp.bfloat16):
    entries = jax.random.normal(rng, shape, jnp.float32) * deviation
    if len(shards) > 0:
        entries = shard_levels(rng, shape, shards, -0.22, 0.18) * entries
    return jnp.clip(entries, min=-bound, max=bound).astype(dtype)


def setup_inputs(seed: int = 0) -> dict:
    key_of = jax.random.split(jax.random.key(seed), 3)
    fields = centred(key_of[0], (K, 3, NODES, NXE, NYE, EZ), 1.0, 6.0, ((3, 16), (4, 8)), jnp.float32)
    velocity = centred(key_of[1], (STEPS, 3, NODES, EZ, NXE, NYE), 0.5, 3.0, ((3, 128),), jnp.float32)
    return {"fields": fields, "velocity": velocity}


STEP_SIZE = 0.025
FLUX_COEF = 3.0
PENALTY = 3.0

def derivative_table():
    points = np.array([-1.0, -1.0 / np.sqrt(5.0), 1.0 / np.sqrt(5.0), 1.0])
    weights_bary = np.ones(4)
    for first in range(4):
        for second in range(4):
            if first != second:
                weights_bary[first] = weights_bary[first] / (points[first] - points[second])
    table = np.zeros((4, 4))
    for first in range(4):
        for second in range(4):
            if first != second:
                table[first, second] = weights_bary[second] / weights_bary[first] / (points[first] - points[second])
        table[first, first] = -np.sum(table[first])
    return jnp.asarray(table.astype(np.float32))

def along(table, block, direction):
    forms = ['pa,kabcxyz->kpbcxyz', 'pb,kabcxyz->kapcxyz', 'pc,kabcxyz->kabpxyz']
    return jnp.einsum(forms[direction], table, block, precision=lax.Precision.HIGHEST)

def cross_speed(speed, field):
    return jnp.stack([speed[1] * field[:, 2] - speed[2] * field[:, 1], speed[2] * field[:, 0] - speed[0] * field[:, 2], speed[0] * field[:, 1] - speed[1] * field[:, 0]], axis=1)

def normal_cross(direction, jump):
    zeros = jnp.zeros_like(jump[:, 0])
    if direction == 0:
        parts = [zeros, -jump[:, 2], jump[:, 1]]
    elif direction == 1:
        parts = [jump[:, 2], zeros, -jump[:, 0]]
    else:
        parts = [-jump[:, 1], jump[:, 0], zeros]
    return jnp.stack(parts, axis=1)

def tendency(field, speed, borders):
    table = derivative_table()
    elec = cross_speed(speed, field)
    result = jnp.stack([along(table, elec[:, 2], 1) - along(table, elec[:, 1], 2), along(table, elec[:, 0], 2) - along(table, elec[:, 2], 0), along(table, elec[:, 1], 0) - along(table, elec[:, 0], 1)], axis=1)
    packed = jnp.concatenate([elec, field], axis=1)
    for direction in range(3):
        node_dim = 2 + direction
        elem_dim = 4 + direction
        lower = lax.index_in_dim(packed, 0, node_dim, keepdims=False)
        upper = lax.index_in_dim(packed, 3, node_dim, keepdims=False)
        recv_low, recv_high = borders(direction, lower, upper)
        count = lower.shape[elem_dim]
        outer_high = jnp.concatenate([lax.slice_in_dim(lower, 1, count, axis=elem_dim), recv_high], axis=elem_dim)
        outer_low = jnp.concatenate([recv_low, lax.slice_in_dim(upper, 0, count - 1, axis=elem_dim)], axis=elem_dim)
        jump_high = outer_high - upper
        jump_low = outer_low - lower
        term_high = FLUX_COEF * normal_cross(direction, jump_high[:, :3]) + PENALTY * jump_high[:, 3:]
        term_low = -FLUX_COEF * normal_cross(direction, jump_low[:, :3]) + PENALTY * jump_low[:, 3:]
        high_index = (slice(None),) * node_dim + (3,)
        low_index = (slice(None),) * node_dim + (0,)
        result = result.at[high_index].add(term_high)
        result = result.at[low_index].add(term_low)
    return result

def advance(field, speed, borders):
    first = tendency(field, speed, borders)
    middle = field + STEP_SIZE * first
    second = tendency(middle, speed, borders)
    return field + 0.5 * STEP_SIZE * (first + second)

def zero_borders(direction, lower, upper):
    empty = jnp.zeros_like(lax.slice_in_dim(lower, 0, 1, axis=4 + direction))
    return (empty, empty)

def reference(fields, velocity):
    speeds = jnp.transpose(velocity, (0, 1, 2, 4, 5, 3)).reshape(STEPS, 3, 4, 4, 4, NXE, NYE, EZ)

    def one_field(field):
        state = field.reshape(1, 3, 4, 4, 4, NXE, NYE, EZ)
        for step in range(STEPS):
            state = advance(state, speeds[step], zero_borders)
        return state.reshape(3, NODES, NXE, NYE, EZ)
    return lax.map(one_field, fields)
```

```python
import jax
import jax.numpy as jnp
import numpy as np
from jax import lax
from jax.experimental import pallas as pl
from jax.experimental.pallas import tpu as pltpu
from jax.sharding import PartitionSpec as P

STEP_SIZE = 0.025
FLUX_COEF = 3.0
KRYLOV = 4
SIDE = 4
LANES = 128
F32 = jnp.float32
VMEM_LIMIT = 24 * 1024 * 1024


def derivative_table():
    points = np.array([-1.0, -1.0 / np.sqrt(5.0), 1.0 / np.sqrt(5.0), 1.0])
    weights_bary = np.ones(4)
    for first in range(4):
        for second in range(4):
            if first != second:
                weights_bary[first] = weights_bary[first] / (points[first] - points[second])
    table = np.zeros((4, 4))
    for first in range(4):
        for second in range(4):
            if first != second:
                table[first, second] = (
                    weights_bary[second] / weights_bary[first] / (points[first] - points[second])
                )
        table[first, first] = -np.sum(table[first])
    return table.astype(np.float32).astype(np.float64)


TABLE = derivative_table()


def rows():
    return lax.broadcasted_iota(jnp.int32, (8, LANES), 0)


def lanes():
    return lax.broadcasted_iota(jnp.int32, (8, LANES), 1)


def roll_rows(value, shift):
    return pltpu.roll(value, shift % 8, 0)


def roll_lanes(value, shift):
    return pltpu.roll(value, shift % LANES, 1)


def cross(u, b):
    return [
        u[1] * b[2] - u[2] * b[1],
        u[2] * b[0] - u[0] * b[2],
        u[0] * b[1] - u[1] * b[0],
    ]


def plus(direction, b, e):
    if direction == 0:
        return [b[0], b[1] - e[2], b[2] + e[1]]
    if direction == 1:
        return [b[0] + e[2], b[1], b[2] - e[0]]
    return [b[0] - e[1], b[1] + e[0], b[2]]


def minus(direction, b, e):
    if direction == 0:
        return [b[0], b[1] + e[2], b[2] - e[1]]
    if direction == 1:
        return [b[0] - e[2], b[1], b[2] + e[0]]
    return [b[0] + e[1], b[1] - e[0], b[2]]


def speed_at(speed, a, b):
    start = (a * SIDE + b) * 8
    return [speed[i, start : start + 8, :] for i in range(3)]


def third_table(coef):
    node = rows() // 2
    parts = []
    for shift in range(SIDE):
        part = jnp.zeros((8, LANES), F32)
        for p in range(SIDE):
            part = jnp.where(node == p, F32(coef * TABLE[p, (p - shift) % SIDE]), part)
        parts.append(part)
    return parts


def weighted(row, terms):
    total = None
    for q in range(SIDE):
        if row[q] != 0.0:
            part = F32(row[q]) * terms[q]
            total = part if total is None else total + part
    return total


def volume(k, state, base, speed, elec, out, coef):
    row, lane = rows(), lanes()
    table = coef * TABLE
    third = third_table(coef)
    jump = FLUX_COEF * coef
    zero = jnp.zeros((8, LANES), F32)
    own_low = jnp.where(row < 2, F32(jump), zero)
    own_high = jnp.where(row >= 6, F32(jump), zero)
    in_low = jnp.where(lane > 0, own_low, zero)
    in_high = jnp.where(lane < LANES - 1, own_high, zero)
    odd = row % 2 == 1
    mid_low = jnp.where(odd, F32(jump), zero)
    mid_high = jnp.where(odd, zero, F32(jump))

    def along_third(value):
        total = third[0] * value
        for shift in range(1, SIDE):
            total = total + third[shift] * roll_rows(value, 2 * shift)
        return total

    for a in range(SIDE):
        for b in range(SIDE):
            field = [state[k, i, a, b] for i in range(3)]
            parts = cross(speed_at(speed, a, b), field)
            for i in range(3):
                elec[i, a, b] = parts[i]
    for a in range(SIDE):
        for b in range(SIDE):
            e = [elec[i, a, b] for i in range(3)]
            m = [state[k, i, a, b] for i in range(3)]
            total = [
                weighted(table[b], [elec[2, a, q] for q in range(SIDE)]) - along_third(e[1]),
                along_third(e[0]) - weighted(table[a], [elec[2, q, b] for q in range(SIDE)]),
                weighted(table[a], [elec[1, q, b] for q in range(SIDE)])
                - weighted(table[b], [elec[0, a, q] for q in range(SIDE)]),
            ]
            up, down = minus(2, m, e), plus(2, m, e)
            for i in range(3):
                total[i] = total[i] - (own_low * up[i] + own_high * down[i])
                total[i] = total[i] + in_low * roll_lanes(roll_rows(up[i], 2), 1)
                total[i] = total[i] + in_high * roll_lanes(roll_rows(down[i], -2), -1)
            if a == 0:
                own = minus(0, m, e)
                total = [t - F32(jump) * o for t, o in zip(total, own)]
            if a == SIDE - 1:
                own = plus(0, m, e)
                total = [t - F32(jump) * o for t, o in zip(total, own)]
            if b == 0:
                own = minus(1, m, e)
                far_b = [state[k, i, a, SIDE - 1] for i in range(3)]
                far_e = [elec[i, a, SIDE - 1] for i in range(3)]
                far = minus(1, far_b, far_e)
                total = [
                    t - F32(jump) * o + mid_low * roll_rows(f, 1)
                    for t, o, f in zip(total, own, far)
                ]
            if b == SIDE - 1:
                own = plus(1, m, e)
                far_b = [state[k, i, a, 0] for i in range(3)]
                far_e = [elec[i, a, 0] for i in range(3)]
                far = plus(1, far_b, far_e)
                total = [
                    t - F32(jump) * o + mid_high * roll_rows(f, -1)
                    for t, o, f in zip(total, own, far)
                ]
            start = base(k, a, b)
            for i in range(3):
                out[k, i, a, b] = start[i] + total[i]


def parities():
    return lax.axis_index("gx") % 2 == 1, lax.axis_index("gy") % 2 == 1


def pick(condition, yes, no):
    return jnp.where(condition, yes, no)


def pack_rows(first, second, keep_odd):
    odd = rows() % 2 == 1
    if keep_odd:
        return jnp.where(odd, second, roll_rows(first, -1))
    return jnp.where(odd, roll_rows(second, 1), first)


def send_faces(k, state, speed, px, py, x_even, x_odd, y_even, y_odd):
    def traces(direction, sign, a, b):
        m = [state[k, i, a, b] for i in range(3)]
        if speed is None:
            return m
        e = cross(speed_at(speed, a, b), m)
        return plus(direction, m, e) if sign > 0 else minus(direction, m, e)

    for b in range(SIDE):
        high = traces(0, -1, SIDE - 1, b)
        low = traces(0, 1, 0, b)
        for i in range(3):
            x_even[k, i, b] = pick(px, low[i], high[i])
            x_odd[k, i, b] = pick(px, high[i], low[i])
    for half in range(2):
        high = [traces(1, -1, 2 * half + s, SIDE - 1) for s in range(2)]
        low = [traces(1, 1, 2 * half + s, 0) for s in range(2)]
        for i in range(3):
            up = pack_rows(high[0][i], high[1][i], True)
            down = pack_rows(low[0][i], low[1][i], False)
            y_even[k, i, half] = pick(py, down, up)
            y_odd[k, i, half] = pick(py, up, down)


def receive_faces(k, pre, out, ghost_speed, px, py, x_even, x_odd, y_even, y_odd, coef):
    jump = FLUX_COEF * coef
    odd = rows() % 2 == 1
    zero = jnp.zeros((8, LANES), F32)
    mask_low = jnp.where(odd, zero, F32(jump))
    mask_high = jnp.where(odd, F32(jump), zero)
    turn = jnp.where(odd, F32(1.0), F32(-1.0))
    for b in range(SIDE):
        low = [pick(px, x_even[k, i, b], x_odd[k, i, b]) for i in range(3)]
        high = [pick(px, x_odd[k, i, b], x_even[k, i, b]) for i in range(3)]
        if ghost_speed is not None:
            u_low = [ghost_speed[i, b * 8 : b * 8 + 8, :] for i in range(3)]
            u_high = [ghost_speed[i, 32 + b * 8 : 40 + b * 8, :] for i in range(3)]
            low = minus(0, low, cross(u_low, low))
            high = plus(0, high, cross(u_high, high))
        for i in range(3):
            out[k, i, 0, b] = pre[k, i, 0, b] + F32(jump) * low[i]
            out[k, i, SIDE - 1, b] = pre[k, i, SIDE - 1, b] + F32(jump) * high[i]
    for a in (1, 2):
        for b in range(SIDE):
            for i in range(3):
                out[k, i, a, b] = pre[k, i, a, b]
    for half in range(2):
        low = [pick(py, y_even[k, i, half], y_odd[k, i, half]) for i in range(3)]
        high = [pick(py, y_odd[k, i, half], y_even[k, i, half]) for i in range(3)]
        for s in range(2):
            a = 2 * half + s
            if s == 0:
                both = [jnp.where(odd, roll_rows(h, 1), l) for l, h in zip(low, high)]
            else:
                both = [jnp.where(odd, h, roll_rows(l, -1)) for l, h in zip(low, high)]
            if ghost_speed is not None:
                u = [ghost_speed[i, 64 + a * 8 : 72 + a * 8, :] for i in range(3)]
                e = cross(u, both)
                both = [both[0] + turn * e[2], both[1], both[2] - turn * e[0]]
            for i in range(3):
                out[k, i, a, 0] = out[k, i, a, 0] + mask_low * both[i]
                out[k, i, a, SIDE - 1] = out[k, i, a, SIDE - 1] + mask_high * both[i]


ROWS = 9


def pack_kernel(velocity, out):
    wide = velocity.shape[1]
    pairs = velocity.shape[2] // 2
    lane = lax.broadcasted_iota(jnp.int32, (pairs, 64), 1)
    upper = lane % 16 >= 12

    def both(q, x):
        return [velocity[q, x, pl.ds(j, pairs, stride=2), :] for j in range(2)]

    def store(x, q, value):
        out[pl.ds(x * pairs * ROWS + q, pairs, stride=ROWS), :] = value

    for x in range(wide):
        for q in range(6):
            store(x, q, jnp.concatenate(both(q, x), axis=1))
        for q in range(3):
            even, odd = both(q, x)
            even_low, odd_low = both(q, (x - 1) % wide)
            even_high, odd_high = both(q, (x + 1) % wide)
            y_part = jnp.where(upper, pltpu.roll(odd, 1, 0), pltpu.roll(even, pairs - 1, 0))
            store(
                x,
                6 + q,
                jnp.concatenate(
                    [
                        y_part,
                        even_high[:, :16],
                        odd_high[:, :16],
                        odd_low[:, 48:],
                        even_low[:, 48:],
                    ],
                    axis=1,
                ),
            )


def faces_kernel(state, x_even, x_odd, y_even, y_odd):
    px, py = parities()

    def step(k, carry):
        send_faces(k, state, None, px, py, x_even, x_odd, y_even, y_odd)
        return carry

    lax.fori_loop(0, KRYLOV, step, 0)


def unpack_kernel(arrived, first, second, ghosts):
    for q in range(ROWS):
        block = arrived[pl.ds(q, LANES, stride=ROWS), :].T
        if q < 6:
            into = first if q < 3 else second
            into[q % 3, pl.ds(0, 64, stride=2), :] = block[:64]
            into[q % 3, pl.ds(1, 64, stride=2), :] = block[64:]
        else:
            i = q - 6
            ghosts[i, pl.ds(0, 16, stride=2), :] = block[112:]
            ghosts[i, pl.ds(1, 16, stride=2), :] = block[96:112]
            ghosts[i, pl.ds(32, 16, stride=2), :] = block[64:80]
            ghosts[i, pl.ds(33, 16, stride=2), :] = block[80:96]
            for a in range(SIDE):
                ghosts[i, pl.ds(64 + a * 8, 4, stride=2), :] = block[a * 16 + 12 : a * 16 + 16]
                ghosts[i, pl.ds(65 + a * 8, 4, stride=2), :] = block[a * 16 : a * 16 + 4]


def first_volume_kernel(state, speed, pre, elec):
    def base(k, a, b):
        return [state[k, i, a, b] for i in range(3)]

    def step(k, carry):
        volume(k, state, base, speed, elec, pre, STEP_SIZE)
        return carry

    lax.fori_loop(0, KRYLOV, step, 0)


def second_volume_kernel(state, start, speed, pre, elec):
    def base(k, a, b):
        return [F32(0.5) * (state[k, i, a, b] + start[k, i, a, b]) for i in range(3)]

    def step(k, carry):
        volume(k, state, base, speed, elec, pre, 0.5 * STEP_SIZE)
        return carry

    lax.fori_loop(0, KRYLOV, step, 0)


def finish_kernel(coef, has_ghosts, has_next, *refs):
    px, py = parities()
    pre, *arrived = refs[:5]
    refs = refs[5:]
    ghosts = speed = None
    if has_ghosts:
        ghosts, refs = refs[0], refs[1:]
    if has_next:
        speed, refs = refs[0], refs[1:]
    out, *leaving = refs

    def step(k, carry):
        receive_faces(k, pre, out, ghosts, px, py, *arrived, coef)
        if has_next:
            send_faces(k, out, speed, px, py, *leaving)
        return carry

    lax.fori_loop(0, KRYLOV, step, 0)


STATE = (KRYLOV, 3, SIDE, SIDE, 8, LANES)
X_FACE = (KRYLOV, 3, SIDE, 8, LANES)
Y_FACE = (KRYLOV, 3, SIDE // 2, 8, LANES)
SPEED = (3, 128, LANES)
GHOSTS = (3, 96, LANES)
FACES = (X_FACE, X_FACE, Y_FACE, Y_FACE)


def call(kernel, shapes, flops, *operands, scratch=()):
    whole = pl.BlockSpec(memory_space=pltpu.VMEM)
    return pl.pallas_call(
        kernel,
        out_shape=[jax.ShapeDtypeStruct(shape, F32) for shape in shapes],
        in_specs=[whole] * len(operands),
        out_specs=[whole] * len(shapes),
        scratch_shapes=[pltpu.VMEM(shape, F32) for shape in scratch],
        compiler_params=pltpu.CompilerParams(vmem_limit_bytes=VMEM_LIMIT),
        cost_estimate=pl.CostEstimate(
            flops=flops, bytes_accessed=2 * 1024 * 1024, transcendentals=0
        ),
    )(*operands)


def exchange(faces):
    received = []
    for index, face in enumerate(faces):
        axis = "gx" if index < 2 else "gy"
        count = lax.axis_size(axis)
        if index % 2 == 0:
            pairs = [(i, i ^ 1) for i in range(count)]
        else:
            pairs = [(i, ((i - 1) ^ 1) + 1) for i in range(1, count - 1)]
        received.append(lax.ppermute(face, axis, pairs))
    return received


def shards(fields, velocity):
    phases, comps, nodes, slab, wide_x, wide_y = velocity.shape
    devices = lax.axis_size("gx") * lax.axis_size("gy")
    state = fields.reshape(STATE)
    layers = jnp.transpose(velocity, (0, 1, 3, 4, 5, 2))
    layers = layers.reshape(phases * comps, wide_x, wide_y, nodes)
    (packed,) = call(pack_kernel, [(devices * ROWS, LANES)], 10**6, layers)
    packed = packed.reshape(devices, ROWS * LANES)
    moved = lax.all_to_all(packed, ("gx", "gy"), split_axis=0, concat_axis=0, tiled=True)
    moved = moved.reshape(devices * ROWS, LANES)
    arrived = exchange(call(faces_kernel, FACES, 10**6, state))
    *speeds, ghosts = call(unpack_kernel, [SPEED, SPEED, GHOSTS], 10**6, moved)
    elec = [(3, SIDE, SIDE, 8, LANES)]
    for phase in range(phases):
        speed = speeds[phase]
        (pre,) = call(first_volume_kernel, [STATE], 10**7, state, speed, scratch=elec)
        if phase == 0:
            extra = (ghosts, speed)
        else:
            extra = (speed,)

        def first_finish(*refs, has_ghosts=phase == 0):
            finish_kernel(STEP_SIZE, has_ghosts, True, *refs)

        middle, *leaving = call(first_finish, [STATE, *FACES], 10**6, pre, *arrived, *extra)
        arrived = exchange(leaving)
        (pre,) = call(second_volume_kernel, [STATE], 10**7, middle, state, speed, scratch=elec)
        has_next = phase + 1 < phases

        def second_finish(*refs, has_next=has_next):
            finish_kernel(0.5 * STEP_SIZE, False, has_next, *refs)

        extra = (speeds[phase + 1],) if has_next else ()
        shapes = [STATE, *FACES] if has_next else [STATE]
        state, *leaving = call(second_finish, shapes, 10**6, pre, *arrived, *extra)
        if has_next:
            arrived = exchange(leaving)
    return state.reshape(fields.shape)


def solution(mesh):
    return jax.shard_map(
        shards,
        mesh=mesh,
        in_specs=(
            P(None, None, None, "gx", "gy", None),
            P(None, None, None, ("gx", "gy"), None, None),
        ),
        out_specs=P(None, None, None, "gx", "gy", None),
        check_vma=False,
    )
```

```python
import jax
import jax.numpy as jnp
import numpy as np
from jax import lax
from jax.experimental import pallas as pl
from jax.experimental.pallas import tpu as pltpu
from jax.sharding import PartitionSpec as P

STEP_SIZE = 0.025
FLUX_COEF = 3.0
KRYLOV = 4
SIDE = 4
LANES = 128
F32 = jnp.float32
VMEM_LIMIT = 24 * 1024 * 1024


def derivative_table():
    points = np.array([-1.0, -1.0 / np.sqrt(5.0), 1.0 / np.sqrt(5.0), 1.0])
    weights_bary = np.ones(4)
    for first in range(4):
        for second in range(4):
            if first != second:
                weights_bary[first] = weights_bary[first] / (points[first] - points[second])
    table = np.zeros((4, 4))
    for first in range(4):
        for second in range(4):
            if first != second:
                table[first, second] = (
                    weights_bary[second] / weights_bary[first] / (points[first] - points[second])
                )
        table[first, first] = -np.sum(table[first])
    return table.astype(np.float32).astype(np.float64)


TABLE = derivative_table()


def rows():
    return lax.broadcasted_iota(jnp.int32, (8, LANES), 0)


def lanes():
    return lax.broadcasted_iota(jnp.int32, (8, LANES), 1)


def roll_rows(value, shift):
    return pltpu.roll(value, shift % 8, 0)


def roll_lanes(value, shift):
    return pltpu.roll(value, shift % LANES, 1)


def cross(u, b):
    return [
        u[1] * b[2] - u[2] * b[1],
        u[2] * b[0] - u[0] * b[2],
        u[0] * b[1] - u[1] * b[0],
    ]


def plus(direction, b, e):
    if direction == 0:
        return [b[0], b[1] - e[2], b[2] + e[1]]
    if direction == 1:
        return [b[0] + e[2], b[1], b[2] - e[0]]
    return [b[0] - e[1], b[1] + e[0], b[2]]


def minus(direction, b, e):
    if direction == 0:
        return [b[0], b[1] + e[2], b[2] - e[1]]
    if direction == 1:
        return [b[0] - e[2], b[1], b[2] + e[0]]
    return [b[0] + e[1], b[1] - e[0], b[2]]


def speed_at(speed, a, b):
    start = (a * SIDE + b) * 8
    return [speed[i, start : start + 8, :] for i in range(3)]


def third_table(coef):
    node = rows() // 2
    parts = []
    for shift in range(SIDE):
        part = jnp.zeros((8, LANES), F32)
        for p in range(SIDE):
            part = jnp.where(node == p, F32(coef * TABLE[p, (p - shift) % SIDE]), part)
        parts.append(part)
    return parts


def weighted(row, terms):
    total = None
    for q in range(SIDE):
        if row[q] != 0.0:
            part = F32(row[q]) * terms[q]
            total = part if total is None else total + part
    return total


def volume(k, state, base, speed, elec, out, coef):
    row, lane = rows(), lanes()
    table = coef * TABLE
    third = third_table(coef)
    jump = FLUX_COEF * coef
    zero = jnp.zeros((8, LANES), F32)
    own_low = jnp.where(row < 2, F32(jump), zero)
    own_high = jnp.where(row >= 6, F32(jump), zero)
    in_low = jnp.where(lane > 0, own_low, zero)
    in_high = jnp.where(lane < LANES - 1, own_high, zero)
    odd = row % 2 == 1
    mid_low = jnp.where(odd, F32(jump), zero)
    mid_high = jnp.where(odd, zero, F32(jump))

    def along_third(value):
        total = third[0] * value
        for shift in range(1, SIDE):
            total = total + third[shift] * roll_rows(value, 2 * shift)
        return total

    for a in range(SIDE):
        for b in range(SIDE):
            field = [state[k, i, a, b] for i in range(3)]
            parts = cross(speed_at(speed, a, b), field)
            for i in range(3):
                elec[i, a, b] = parts[i]
    for a in range(SIDE):
        for b in range(SIDE):
            e = [elec[i, a, b] for i in range(3)]
            m = [state[k, i, a, b] for i in range(3)]
            total = [
                weighted(table[b], [elec[2, a, q] for q in range(SIDE)]) - along_third(e[1]),
                along_third(e[0]) - weighted(table[a], [elec[2, q, b] for q in range(SIDE)]),
                weighted(table[a], [elec[1, q, b] for q in range(SIDE)])
                - weighted(table[b], [elec[0, a, q] for q in range(SIDE)]),
            ]
            up, down = minus(2, m, e), plus(2, m, e)
            for i in range(3):
                total[i] = total[i] - (own_low * up[i] + own_high * down[i])
                total[i] = total[i] + in_low * roll_lanes(roll_rows(up[i], 2), 1)
                total[i] = total[i] + in_high * roll_lanes(roll_rows(down[i], -2), -1)
            if a == 0:
                own = minus(0, m, e)
                total = [t - F32(jump) * o for t, o in zip(total, own)]
            if a == SIDE - 1:
                own = plus(0, m, e)
                total = [t - F32(jump) * o for t, o in zip(total, own)]
            if b == 0:
                own = minus(1, m, e)
                far_b = [state[k, i, a, SIDE - 1] for i in range(3)]
                far_e = [elec[i, a, SIDE - 1] for i in range(3)]
                far = minus(1, far_b, far_e)
                total = [
                    t - F32(jump) * o + mid_low * roll_rows(f, 1)
                    for t, o, f in zip(total, own, far)
                ]
            if b == SIDE - 1:
                own = plus(1, m, e)
                far_b = [state[k, i, a, 0] for i in range(3)]
                far_e = [elec[i, a, 0] for i in range(3)]
                far = plus(1, far_b, far_e)
                total = [
                    t - F32(jump) * o + mid_high * roll_rows(f, -1)
                    for t, o, f in zip(total, own, far)
                ]
            start = base(k, a, b)
            for i in range(3):
                out[k, i, a, b] = start[i] + total[i]


def parities():
    return lax.axis_index("gx") % 2 == 1, lax.axis_index("gy") % 2 == 1


def pick(condition, yes, no):
    return jnp.where(condition, yes, no)


def pack_rows(first, second, keep_odd):
    odd = rows() % 2 == 1
    if keep_odd:
        return jnp.where(odd, second, roll_rows(first, -1))
    return jnp.where(odd, roll_rows(second, 1), first)


def send_faces(k, state, speed, px, py, y_even, x_odd, y_odd, x_even):
    def traces(direction, sign, a, b):
        m = [state[k, i, a, b] for i in range(3)]
        if speed is None:
            return m
        e = cross(speed_at(speed, a, b), m)
        return plus(direction, m, e) if sign > 0 else minus(direction, m, e)

    for b in range(SIDE):
        high = traces(0, -1, SIDE - 1, b)
        low = traces(0, 1, 0, b)
        for i in range(3):
            x_even[k, i, b] = pick(px, low[i], high[i])
            x_odd[k, i, b] = pick(px, high[i], low[i])
    for half in range(2):
        high = [traces(1, -1, 2 * half + s, SIDE - 1) for s in range(2)]
        low = [traces(1, 1, 2 * half + s, 0) for s in range(2)]
        for i in range(3):
            up = pack_rows(high[0][i], high[1][i], True)
            down = pack_rows(low[0][i], low[1][i], False)
            y_even[k, i, half] = pick(py, down, up)
            y_odd[k, i, half] = pick(py, up, down)


def receive_faces(k, pre, out, ghost_speed, px, py, y_even, x_odd, y_odd, x_even, coef):
    jump = FLUX_COEF * coef
    odd = rows() % 2 == 1
    zero = jnp.zeros((8, LANES), F32)
    mask_low = jnp.where(odd, zero, F32(jump))
    mask_high = jnp.where(odd, F32(jump), zero)
    turn = jnp.where(odd, F32(1.0), F32(-1.0))
    for b in range(SIDE):
        low = [pick(px, x_even[k, i, b], x_odd[k, i, b]) for i in range(3)]
        high = [pick(px, x_odd[k, i, b], x_even[k, i, b]) for i in range(3)]
        if ghost_speed is not None:
            u_low = [ghost_speed[i, b * 8 : b * 8 + 8, :] for i in range(3)]
            u_high = [ghost_speed[i, 32 + b * 8 : 40 + b * 8, :] for i in range(3)]
            low = minus(0, low, cross(u_low, low))
            high = plus(0, high, cross(u_high, high))
        for i in range(3):
            out[k, i, 0, b] = pre[k, i, 0, b] + F32(jump) * low[i]
            out[k, i, SIDE - 1, b] = pre[k, i, SIDE - 1, b] + F32(jump) * high[i]
    for a in (1, 2):
        for b in range(SIDE):
            for i in range(3):
                out[k, i, a, b] = pre[k, i, a, b]
    for half in range(2):
        low = [pick(py, y_even[k, i, half], y_odd[k, i, half]) for i in range(3)]
        high = [pick(py, y_odd[k, i, half], y_even[k, i, half]) for i in range(3)]
        for s in range(2):
            a = 2 * half + s
            if s == 0:
                both = [jnp.where(odd, roll_rows(h, 1), l) for l, h in zip(low, high)]
            else:
                both = [jnp.where(odd, h, roll_rows(l, -1)) for l, h in zip(low, high)]
            if ghost_speed is not None:
                u = [ghost_speed[i, 64 + a * 8 : 72 + a * 8, :] for i in range(3)]
                e = cross(u, both)
                both = [both[0] + turn * e[2], both[1], both[2] - turn * e[0]]
            for i in range(3):
                out[k, i, a, 0] = out[k, i, a, 0] + mask_low * both[i]
                out[k, i, a, SIDE - 1] = out[k, i, a, SIDE - 1] + mask_high * both[i]


ROWS = 9


def pack_kernel(velocity, out):
    wide = velocity.shape[1]
    pairs = velocity.shape[2] // 2
    lane = lax.broadcasted_iota(jnp.int32, (pairs, 64), 1)
    upper = lane % 16 >= 12

    def both(q, x):
        return [velocity[q, x, pl.ds(j, pairs, stride=2), :] for j in range(2)]

    def store(x, q, value):
        out[pl.ds(x * pairs * ROWS + q, pairs, stride=ROWS), :] = value

    for x in range(wide):
        for q in range(6):
            store(x, q, jnp.concatenate(both(q, x), axis=1))
        for q in range(3):
            even, odd = both(q, x)
            even_low, odd_low = both(q, (x - 1) % wide)
            even_high, odd_high = both(q, (x + 1) % wide)
            y_part = jnp.where(upper, pltpu.roll(odd, 1, 0), pltpu.roll(even, pairs - 1, 0))
            store(
                x,
                6 + q,
                jnp.concatenate(
                    [
                        y_part,
                        even_high[:, :16],
                        odd_high[:, :16],
                        odd_low[:, 48:],
                        even_low[:, 48:],
                    ],
                    axis=1,
                ),
            )


def faces_kernel(state, y_even, x_odd, y_odd, x_even):
    px, py = parities()

    def step(k, carry):
        send_faces(k, state, None, px, py, y_even, x_odd, y_odd, x_even)
        return carry

    lax.fori_loop(0, KRYLOV, step, 0)


def unpack_kernel(arrived, first, second, ghosts):
    for q in range(ROWS):
        block = arrived[pl.ds(q, LANES, stride=ROWS), :].T
        if q < 6:
            into = first if q < 3 else second
            into[q % 3, pl.ds(0, 64, stride=2), :] = block[:64]
            into[q % 3, pl.ds(1, 64, stride=2), :] = block[64:]
        else:
            i = q - 6
            ghosts[i, pl.ds(0, 16, stride=2), :] = block[112:]
            ghosts[i, pl.ds(1, 16, stride=2), :] = block[96:112]
            ghosts[i, pl.ds(32, 16, stride=2), :] = block[64:80]
            ghosts[i, pl.ds(33, 16, stride=2), :] = block[80:96]
            for a in range(SIDE):
                ghosts[i, pl.ds(64 + a * 8, 4, stride=2), :] = block[a * 16 + 12 : a * 16 + 16]
                ghosts[i, pl.ds(65 + a * 8, 4, stride=2), :] = block[a * 16 : a * 16 + 4]


def first_volume_kernel(state, speed, pre, elec):
    def base(k, a, b):
        return [state[k, i, a, b] for i in range(3)]

    def step(k, carry):
        volume(k, state, base, speed, elec, pre, STEP_SIZE)
        return carry

    lax.fori_loop(0, KRYLOV, step, 0)


def second_volume_kernel(state, start, speed, pre, elec):
    def base(k, a, b):
        return [F32(0.5) * (state[k, i, a, b] + start[k, i, a, b]) for i in range(3)]

    def step(k, carry):
        volume(k, state, base, speed, elec, pre, 0.5 * STEP_SIZE)
        return carry

    lax.fori_loop(0, KRYLOV, step, 0)


def finish_kernel(coef, has_ghosts, has_next, *refs):
    px, py = parities()
    pre, *arrived = refs[:5]
    refs = refs[5:]
    ghosts = speed = None
    if has_ghosts:
        ghosts, refs = refs[0], refs[1:]
    if has_next:
        speed, refs = refs[0], refs[1:]
    out, *leaving = refs

    def step(k, carry):
        receive_faces(k, pre, out, ghosts, px, py, *arrived, coef)
        if has_next:
            send_faces(k, out, speed, px, py, *leaving)
        return carry

    lax.fori_loop(0, KRYLOV, step, 0)


STATE = (KRYLOV, 3, SIDE, SIDE, 8, LANES)
X_FACE = (KRYLOV, 3, SIDE, 8, LANES)
Y_FACE = (KRYLOV, 3, SIDE // 2, 8, LANES)
SPEED = (3, 128, LANES)
GHOSTS = (3, 96, LANES)
FACES = (Y_FACE, X_FACE, Y_FACE, X_FACE)
ORDER = ('y_even', 'x_odd', 'y_odd', 'x_even')


def call(kernel, shapes, flops, *operands, scratch=()):
    whole = pl.BlockSpec(memory_space=pltpu.VMEM)
    return pl.pallas_call(
        kernel,
        out_shape=[jax.ShapeDtypeStruct(shape, F32) for shape in shapes],
        in_specs=[whole] * len(operands),
        out_specs=[whole] * len(shapes),
        scratch_shapes=[pltpu.VMEM(shape, F32) for shape in scratch],
        compiler_params=pltpu.CompilerParams(vmem_limit_bytes=VMEM_LIMIT),
        cost_estimate=pl.CostEstimate(
            flops=flops, bytes_accessed=2 * 1024 * 1024, transcendentals=0
        ),
    )(*operands)


WAITS = (("y_even", 2 * 10**9), ("x_odd", 10**10))


def exchange(faces, waits=WAITS):
    received = []
    for index, face in enumerate(faces):
        axis = "gx" if ORDER[index][0] == "x" else "gy"
        count = lax.axis_size(axis)
        if ORDER[index][2:] == "even":
            pairs = [(i, i ^ 1) for i in range(count)]
        else:
            pairs = [(i, ((i - 1) ^ 1) + 1) for i in range(1, count - 1)]
        received.append(lax.ppermute(face, axis, pairs))
    return in_order(received, waits)


def pass_kernel(arrived, *refs):
    refs[-1][...] = arrived[...]


def in_order(received, waits):
    whole = pl.BlockSpec(memory_space=pltpu.VMEM)
    before = ()
    for name, flops in waits:
        index = ORDER.index(name)
        array = received[index]
        received[index] = pl.pallas_call(
            pass_kernel,
            out_shape=jax.ShapeDtypeStruct(array.shape, F32),
            in_specs=[whole] + [pl.BlockSpec(memory_space=pl.ANY)] * len(before),
            out_specs=whole,
            compiler_params=pltpu.CompilerParams(vmem_limit_bytes=VMEM_LIMIT),
            cost_estimate=pl.CostEstimate(
                flops=flops, bytes_accessed=flops // 100, transcendentals=0
            ),
        )(array, *before)
        before = (received[index],)
    return received


def shards(fields, velocity):
    phases, comps, nodes, slab, wide_x, wide_y = velocity.shape
    devices = lax.axis_size("gx") * lax.axis_size("gy")
    state = fields.reshape(STATE)
    layers = jnp.transpose(velocity, (0, 1, 3, 4, 5, 2))
    layers = layers.reshape(phases * comps, wide_x, wide_y, nodes)
    (packed,) = call(pack_kernel, [(devices * ROWS, LANES)], 10**6, layers)
    packed = packed.reshape(devices, ROWS * LANES)
    moved = lax.all_to_all(packed, ("gx", "gy"), split_axis=0, concat_axis=0, tiled=True)
    moved = moved.reshape(devices * ROWS, LANES)
    arrived = exchange(call(faces_kernel, FACES, 10**6, state), ())
    *speeds, ghosts = call(unpack_kernel, [SPEED, SPEED, GHOSTS], 10**6, moved)
    elec = [(3, SIDE, SIDE, 8, LANES)]
    for phase in range(phases):
        speed = speeds[phase]
        (pre,) = call(first_volume_kernel, [STATE], 10**7, state, speed, scratch=elec)
        if phase == 0:
            extra = (ghosts, speed)
        else:
            extra = (speed,)

        def first_finish(*refs, has_ghosts=phase == 0):
            finish_kernel(STEP_SIZE, has_ghosts, True, *refs)

        middle, *leaving = call(first_finish, [STATE, *FACES], 10**6, pre, *arrived, *extra)
        arrived = exchange(leaving)
        (pre,) = call(second_volume_kernel, [STATE], 10**7, middle, state, speed, scratch=elec)
        has_next = phase + 1 < phases

        def second_finish(*refs, has_next=has_next):
            finish_kernel(0.5 * STEP_SIZE, False, has_next, *refs)

        extra = (speeds[phase + 1],) if has_next else ()
        shapes = [STATE, *FACES] if has_next else [STATE]
        state, *leaving = call(second_finish, shapes, 10**6, pre, *arrived, *extra)
        if has_next:
            arrived = exchange(leaving)
    return state.reshape(fields.shape)


def solution(mesh):
    return jax.shard_map(
        shards,
        mesh=mesh,
        in_specs=(
            P(None, None, None, "gx", "gy", None),
            P(None, None, None, ("gx", "gy"), None, None),
        ),
        out_specs=P(None, None, None, "gx", "gy", None),
        check_vma=False,
    )
```

```python
import jax
import jax.numpy as jnp
import numpy as np
from jax import lax
from jax.experimental import pallas as pl
from jax.experimental.pallas import tpu as pltpu
from jax.sharding import PartitionSpec as P

STEP_SIZE = 0.025
FLUX_COEF = 3.0
KRYLOV = 4
SIDE = 4
LANES = 128
F32 = jnp.float32
VMEM_LIMIT = 24 * 1024 * 1024


def derivative_table():
    points = np.array([-1.0, -1.0 / np.sqrt(5.0), 1.0 / np.sqrt(5.0), 1.0])
    weights_bary = np.ones(4)
    for first in range(4):
        for second in range(4):
            if first != second:
                weights_bary[first] = weights_bary[first] / (points[first] - points[second])
    table = np.zeros((4, 4))
    for first in range(4):
        for second in range(4):
            if first != second:
                table[first, second] = (
                    weights_bary[second] / weights_bary[first] / (points[first] - points[second])
                )
        table[first, first] = -np.sum(table[first])
    return table.astype(np.float32).astype(np.float64)


TABLE = derivative_table()


def rows():
    return lax.broadcasted_iota(jnp.int32, (8, LANES), 0)


def lanes():
    return lax.broadcasted_iota(jnp.int32, (8, LANES), 1)


def roll_rows(value, shift):
    return pltpu.roll(value, shift % 8, 0)


def roll_lanes(value, shift):
    return pltpu.roll(value, shift % LANES, 1)


def cross(u, b):
    return [
        u[1] * b[2] - u[2] * b[1],
        u[2] * b[0] - u[0] * b[2],
        u[0] * b[1] - u[1] * b[0],
    ]


def plus(direction, b, e):
    if direction == 0:
        return [b[0], b[1] - e[2], b[2] + e[1]]
    if direction == 1:
        return [b[0] + e[2], b[1], b[2] - e[0]]
    return [b[0] - e[1], b[1] + e[0], b[2]]


def minus(direction, b, e):
    if direction == 0:
        return [b[0], b[1] + e[2], b[2] - e[1]]
    if direction == 1:
        return [b[0] - e[2], b[1], b[2] + e[0]]
    return [b[0] + e[1], b[1] - e[0], b[2]]


def speed_at(speed, a, b):
    start = (a * SIDE + b) * 8
    return [speed[i, start : start + 8, :] for i in range(3)]


def third_table(coef):
    node = rows() // 2
    parts = []
    for shift in range(SIDE):
        part = jnp.zeros((8, LANES), F32)
        for p in range(SIDE):
            part = jnp.where(node == p, F32(coef * TABLE[p, (p - shift) % SIDE]), part)
        parts.append(part)
    return parts


def weighted(row, terms):
    total = None
    for q in range(SIDE):
        if row[q] != 0.0:
            part = F32(row[q]) * terms[q]
            total = part if total is None else total + part
    return total


def volume(k, state, base, speed, elec, out, coef):
    row, lane = rows(), lanes()
    table = coef * TABLE
    third = third_table(coef)
    jump = FLUX_COEF * coef
    zero = jnp.zeros((8, LANES), F32)
    own_low = jnp.where(row < 2, F32(jump), zero)
    own_high = jnp.where(row >= 6, F32(jump), zero)
    in_low = jnp.where(lane > 0, own_low, zero)
    in_high = jnp.where(lane < LANES - 1, own_high, zero)
    odd = row % 2 == 1
    mid_low = jnp.where(odd, F32(jump), zero)
    mid_high = jnp.where(odd, zero, F32(jump))

    def along_third(value):
        total = third[0] * value
        for shift in range(1, SIDE):
            total = total + third[shift] * roll_rows(value, 2 * shift)
        return total

    for a in range(SIDE):
        for b in range(SIDE):
            field = [state[k, i, a, b] for i in range(3)]
            parts = cross(speed_at(speed, a, b), field)
            for i in range(3):
                elec[i, a, b] = parts[i]
    for a in range(SIDE):
        for b in range(SIDE):
            e = [elec[i, a, b] for i in range(3)]
            m = [state[k, i, a, b] for i in range(3)]
            total = [
                weighted(table[b], [elec[2, a, q] for q in range(SIDE)]) - along_third(e[1]),
                along_third(e[0]) - weighted(table[a], [elec[2, q, b] for q in range(SIDE)]),
                weighted(table[a], [elec[1, q, b] for q in range(SIDE)])
                - weighted(table[b], [elec[0, a, q] for q in range(SIDE)]),
            ]
            up, down = minus(2, m, e), plus(2, m, e)
            for i in range(3):
                total[i] = total[i] - (own_low * up[i] + own_high * down[i])
                total[i] = total[i] + in_low * roll_lanes(roll_rows(up[i], 2), 1)
                total[i] = total[i] + in_high * roll_lanes(roll_rows(down[i], -2), -1)
            if a == 0:
                own = minus(0, m, e)
                total = [t - F32(jump) * o for t, o in zip(total, own)]
            if a == SIDE - 1:
                own = plus(0, m, e)
                total = [t - F32(jump) * o for t, o in zip(total, own)]
            if b == 0:
                own = minus(1, m, e)
                far_b = [state[k, i, a, SIDE - 1] for i in range(3)]
                far_e = [elec[i, a, SIDE - 1] for i in range(3)]
                far = minus(1, far_b, far_e)
                total = [
                    t - F32(jump) * o + mid_low * roll_rows(f, 1)
                    for t, o, f in zip(total, own, far)
                ]
            if b == SIDE - 1:
                own = plus(1, m, e)
                far_b = [state[k, i, a, 0] for i in range(3)]
                far_e = [elec[i, a, 0] for i in range(3)]
                far = plus(1, far_b, far_e)
                total = [
                    t - F32(jump) * o + mid_high * roll_rows(f, -1)
                    for t, o, f in zip(total, own, far)
                ]
            start = base(k, a, b)
            for i in range(3):
                out[k, i, a, b] = start[i] + total[i]


def parities():
    return lax.axis_index("gx") % 2 == 1, lax.axis_index("gy") % 2 == 1


def pick(condition, yes, no):
    return jnp.where(condition, yes, no)


def pack_rows(first, second, keep_odd):
    odd = rows() % 2 == 1
    if keep_odd:
        return jnp.where(odd, second, roll_rows(first, -1))
    return jnp.where(odd, roll_rows(second, 1), first)


class Form:
    def __init__(self, short):
        self.short = short
        self.x_count, self.y_count = (10, 5) if short else (12, 6)

    def shapes(self):
        x = (KRYLOV, self.x_count, 8, LANES)
        y = (KRYLOV, self.y_count, 8, LANES)
        return [y if name[0] == "y" else x for name in ORDER]

    def x_slot(self, i, b):
        if not self.short:
            return i * SIDE + b
        if i > 0:
            return (i - 1) * SIDE + b
        return {0: 8, SIDE - 1: 9}.get(b)

    def y_slots(self):
        pairs = [(i, 2 * half, 2 * half + 1) for i in range(3) for half in range(2)]
        if self.short:
            pairs = [p for p in pairs if p[0] != 1] + [(1, 0, SIDE - 1)]
        return pairs


ORDER = ("y_even", "x_odd", "y_odd", "x_even")
FULL, SHORT = Form(False), Form(True)


def send_faces(k, form, state, speed, px, py, y_even, x_odd, y_odd, x_even):
    def traces(direction, sign, a, b):
        m = [state[k, i, a, b] for i in range(3)]
        if speed is None:
            return m
        e = cross(speed_at(speed, a, b), m)
        return plus(direction, m, e) if sign > 0 else minus(direction, m, e)

    for b in range(SIDE):
        high = traces(0, -1, SIDE - 1, b)
        low = traces(0, 1, 0, b)
        for i in range(3):
            slot = form.x_slot(i, b)
            if slot is not None:
                x_even[k, slot] = pick(px, low[i], high[i])
                x_odd[k, slot] = pick(px, high[i], low[i])
    high = [traces(1, -1, a, SIDE - 1) for a in range(SIDE)]
    low = [traces(1, 1, a, 0) for a in range(SIDE)]
    for slot, (i, first, second) in enumerate(form.y_slots()):
        up = pack_rows(high[first][i], high[second][i], True)
        down = pack_rows(low[first][i], low[second][i], False)
        y_even[k, slot] = pick(py, down, up)
        y_odd[k, slot] = pick(py, up, down)


class Arrived:
    def __init__(self, form, faces, inner, px, py):
        self.form, self.inner, self.px, self.py = form, inner, px, py
        self.y_even, self.x_odd, self.y_odd, self.x_even = faces

    def x(self, k, side, i, b):
        slot = self.form.x_slot(i, b)
        if slot is None:
            return self.inner[0][k, side, b - 1]
        even, odd = self.x_even[k, slot], self.x_odd[k, slot]
        return pick(self.px, even, odd) if side == 0 else pick(self.px, odd, even)

    def y(self, k, i, a):
        odd_row = rows() % 2 == 1
        for slot, (comp, first, second) in enumerate(self.form.y_slots()):
            if comp == i and a in (first, second):
                even, odd = self.y_even[k, slot], self.y_odd[k, slot]
                low, high = pick(self.py, even, odd), pick(self.py, odd, even)
                if a == first:
                    return jnp.where(odd_row, roll_rows(high, 1), low)
                return jnp.where(odd_row, high, roll_rows(low, -1))
        return self.inner[1][k, a - 1]


def ghost_at(ghost_speed, place):
    return [ghost_speed[i, place * 8 : place * 8 + 8, :] for i in range(3)]


def receive_faces(k, pre, out, ghost_speed, arrived, coef):
    jump = FLUX_COEF * coef
    odd = rows() % 2 == 1
    zero = jnp.zeros((8, LANES), F32)
    mask_low = jnp.where(odd, zero, F32(jump))
    mask_high = jnp.where(odd, F32(jump), zero)
    turn = jnp.where(odd, F32(1.0), F32(-1.0))
    for b in range(SIDE):
        low = [arrived.x(k, 0, i, b) for i in range(3)]
        high = [arrived.x(k, 1, i, b) for i in range(3)]
        if ghost_speed is not None:
            low = minus(0, low, cross(ghost_at(ghost_speed, b), low))
            high = plus(0, high, cross(ghost_at(ghost_speed, SIDE + b), high))
        for i in range(3):
            out[k, i, 0, b] = pre[k, i, 0, b] + F32(jump) * low[i]
            out[k, i, SIDE - 1, b] = pre[k, i, SIDE - 1, b] + F32(jump) * high[i]
    for a in (1, 2):
        for b in range(SIDE):
            for i in range(3):
                out[k, i, a, b] = pre[k, i, a, b]
    for a in range(SIDE):
        both = [arrived.y(k, i, a) for i in range(3)]
        if ghost_speed is not None:
            e = cross(ghost_at(ghost_speed, 2 * SIDE + a), both)
            both = [both[0] + turn * e[2], both[1], both[2] - turn * e[0]]
        for i in range(3):
            out[k, i, a, 0] = out[k, i, a, 0] + mask_low * both[i]
            out[k, i, a, SIDE - 1] = out[k, i, a, SIDE - 1] + mask_high * both[i]


def inside(k, state, now, before, ghost_speed, inner_x, inner_y, coef):
    row, lane = rows(), lanes()
    table = coef * TABLE
    third = third_table(coef)
    jump = FLUX_COEF * coef
    zero = jnp.zeros((8, LANES), F32)
    own_low = jnp.where(row < 2, F32(jump), zero)
    own_high = jnp.where(row >= 6, F32(jump), zero)
    in_low = jnp.where(lane > 0, own_low, zero)
    in_high = jnp.where(lane < LANES - 1, own_high, zero)
    odd = row % 2 == 1
    at_x, at_y = lax.axis_index("gx"), lax.axis_index("gy")
    last_x, last_y = lax.axis_size("gx") - 1, lax.axis_size("gy") - 1

    def along_third(value):
        total = third[0] * value
        for shift in range(1, SIDE):
            total = total + third[shift] * roll_rows(value, 2 * shift)
        return total

    def ends(up, down):
        total = in_low * roll_lanes(roll_rows(up, 2), 1) - own_low * up
        return total + in_high * roll_lanes(roll_rows(down, -2), -1) - own_high * down

    def start(value, old):
        return value if old is None else F32(0.5) * (value + old)

    for side in range(2):
        there = at_x > 0 if side == 0 else at_x < last_x
        m = [[now.x(k, side, i, b) for i in range(3)] for b in range(SIDE)]
        e = [cross(ghost_at(ghost_speed, side * SIDE + b), m[b]) for b in range(SIDE)]
        for b in (1, 2):
            own = m[b][0]
            total = weighted(table[b], [e[q][2] for q in range(SIDE)]) - along_third(e[b][1])
            total = total + ends(own + e[b][1], own - e[b][1])
            total = total + F32(jump) * (state[k, 0, (SIDE - 1) * side, b] - own)
            old = None if before is None else before.x(k, side, 0, b)
            inner_x[k, side, b - 1] = pick(there, start(own, old) + total, zero)
    m = [[now.y(k, i, a) for i in range(3)] for a in range(SIDE)]
    e = [cross(ghost_at(ghost_speed, 2 * SIDE + a), m[a]) for a in range(SIDE)]
    for a in (1, 2):
        own = m[a][1]
        total = along_third(e[a][0]) - weighted(table[a], [e[q][2] for q in range(SIDE)])
        total = total + ends(own - e[a][0], own + e[a][0])
        mine = jnp.where(odd, state[k, 1, a, SIDE - 1], state[k, 1, a, 0])
        total = total + F32(jump) * (mine - own)
        old = None if before is None else before.y(k, 1, a)
        value = start(own, old) + total
        low = pick(at_y > 0, value, zero)
        high = pick(at_y < last_y, value, zero)
        inner_y[k, a - 1] = jnp.where(odd, high, low)


ROWS = 9


def pack_kernel(velocity, out):
    wide = velocity.shape[1]
    pairs = velocity.shape[2] // 2
    lane = lax.broadcasted_iota(jnp.int32, (pairs, 64), 1)
    upper = lane % 16 >= 12

    def both(q, x):
        return [velocity[q, x, pl.ds(j, pairs, stride=2), :] for j in range(2)]

    def store(x, q, value):
        out[pl.ds(x * pairs * ROWS + q, pairs, stride=ROWS), :] = value

    for x in range(wide):
        for q in range(6):
            store(x, q, jnp.concatenate(both(q, x), axis=1))
        for q in range(3):
            even, odd = both(q, x)
            even_low, odd_low = both(q, (x - 1) % wide)
            even_high, odd_high = both(q, (x + 1) % wide)
            y_part = jnp.where(upper, pltpu.roll(odd, 1, 0), pltpu.roll(even, pairs - 1, 0))
            store(
                x,
                6 + q,
                jnp.concatenate(
                    [
                        y_part,
                        even_high[:, :16],
                        odd_high[:, :16],
                        odd_low[:, 48:],
                        even_low[:, 48:],
                    ],
                    axis=1,
                ),
            )


def faces_kernel(state, *faces):
    px, py = parities()

    def step(k, carry):
        send_faces(k, FULL, state, None, px, py, *faces)
        return carry

    lax.fori_loop(0, KRYLOV, step, 0)


def unpack_kernel(arrived, first, second, ghosts):
    for q in range(ROWS):
        block = arrived[pl.ds(q, LANES, stride=ROWS), :].T
        if q < 6:
            into = first if q < 3 else second
            into[q % 3, pl.ds(0, 64, stride=2), :] = block[:64]
            into[q % 3, pl.ds(1, 64, stride=2), :] = block[64:]
        else:
            i = q - 6
            ghosts[i, pl.ds(0, 16, stride=2), :] = block[112:]
            ghosts[i, pl.ds(1, 16, stride=2), :] = block[96:112]
            ghosts[i, pl.ds(32, 16, stride=2), :] = block[64:80]
            ghosts[i, pl.ds(33, 16, stride=2), :] = block[80:96]
            for a in range(SIDE):
                ghosts[i, pl.ds(64 + a * 8, 4, stride=2), :] = block[a * 16 + 12 : a * 16 + 16]
                ghosts[i, pl.ds(65 + a * 8, 4, stride=2), :] = block[a * 16 : a * 16 + 4]


def first_volume_kernel(state, speed, pre, elec):
    def base(k, a, b):
        return [state[k, i, a, b] for i in range(3)]

    def step(k, carry):
        volume(k, state, base, speed, elec, pre, STEP_SIZE)
        return carry

    lax.fori_loop(0, KRYLOV, step, 0)


def second_volume_kernel(state, start, speed, pre, elec):
    def base(k, a, b):
        return [F32(0.5) * (state[k, i, a, b] + start[k, i, a, b]) for i in range(3)]

    def step(k, carry):
        volume(k, state, base, speed, elec, pre, 0.5 * STEP_SIZE)
        return carry

    lax.fori_loop(0, KRYLOV, step, 0)


def inside_kernel(coef, forms, *refs):
    px, py = parities()
    state, ghost_speed, *refs, inner_x, inner_y = refs
    stages = []
    for form in forms:
        faces, refs = refs[:4], refs[4:]
        inner = None
        if form.short:
            inner, refs = refs[:2], refs[2:]
        stages.append(Arrived(form, faces, inner, px, py))
    now = stages[0]
    before = stages[1] if len(stages) > 1 else None

    def step(k, carry):
        inside(k, state, now, before, ghost_speed, inner_x, inner_y, coef)
        return carry

    lax.fori_loop(0, KRYLOV, step, 0)


def finish_kernel(coef, form, has_ghosts, next_form, next_speed, *refs):
    px, py = parities()
    pre, *refs = refs
    faces, refs = refs[:4], refs[4:]
    inner = ghosts = speed = None
    if form.short:
        inner, refs = refs[:2], refs[2:]
    if has_ghosts:
        ghosts, *refs = refs
    if next_speed:
        speed, *refs = refs
    out, *leaving = refs
    arrived = Arrived(form, faces, inner, px, py)

    def step(k, carry):
        receive_faces(k, pre, out, ghosts, arrived, coef)
        if next_form is not None:
            send_faces(k, next_form, out, speed, px, py, *leaving)
        return carry

    lax.fori_loop(0, KRYLOV, step, 0)


STATE = (KRYLOV, 3, SIDE, SIDE, 8, LANES)
INNER = [(KRYLOV, 2, 2, 8, LANES), (KRYLOV, 2, 8, LANES)]
SPEED = (3, 128, LANES)
GHOSTS = (3, 96, LANES)


def call(kernel, shapes, flops, *operands, scratch=()):
    whole = pl.BlockSpec(memory_space=pltpu.VMEM)
    return pl.pallas_call(
        kernel,
        out_shape=[jax.ShapeDtypeStruct(shape, F32) for shape in shapes],
        in_specs=[whole] * len(operands),
        out_specs=[whole] * len(shapes),
        scratch_shapes=[pltpu.VMEM(shape, F32) for shape in scratch],
        compiler_params=pltpu.CompilerParams(vmem_limit_bytes=VMEM_LIMIT),
        cost_estimate=pl.CostEstimate(
            flops=flops, bytes_accessed=2 * 1024 * 1024, transcendentals=0
        ),
    )(*operands)


WAITS = (("y_even", 15 * 10**8), ("x_odd", 10**10))


def exchange(faces, waits=WAITS):
    received = []
    for index, face in enumerate(faces):
        axis = "gx" if ORDER[index][0] == "x" else "gy"
        count = lax.axis_size(axis)
        if ORDER[index][2:] == "even":
            pairs = [(i, i ^ 1) for i in range(count)]
        else:
            pairs = [(i, ((i - 1) ^ 1) + 1) for i in range(1, count - 1)]
        received.append(lax.ppermute(face, axis, pairs))
    return in_order(received, waits)


def pass_kernel(arrived, *refs):
    refs[-1][...] = arrived[...]


def in_order(received, waits):
    whole = pl.BlockSpec(memory_space=pltpu.VMEM)
    before = ()
    for name, flops in waits:
        index = ORDER.index(name)
        array = received[index]
        received[index] = pl.pallas_call(
            pass_kernel,
            out_shape=jax.ShapeDtypeStruct(array.shape, F32),
            in_specs=[whole] + [pl.BlockSpec(memory_space=pl.ANY)] * len(before),
            out_specs=whole,
            compiler_params=pltpu.CompilerParams(vmem_limit_bytes=VMEM_LIMIT),
            cost_estimate=pl.CostEstimate(
                flops=flops, bytes_accessed=flops // 100, transcendentals=0
            ),
        )(array, *before)
        before = (received[index],)
    return received


def shards(fields, velocity):
    phases, comps, nodes, slab, wide_x, wide_y = velocity.shape
    devices = lax.axis_size("gx") * lax.axis_size("gy")
    state = fields.reshape(STATE)
    layers = jnp.transpose(velocity, (0, 1, 3, 4, 5, 2))
    layers = layers.reshape(phases * comps, wide_x, wide_y, nodes)
    (packed,) = call(pack_kernel, [(devices * ROWS, LANES)], 10**6, layers)
    packed = packed.reshape(devices, ROWS * LANES)
    moved = lax.all_to_all(packed, ("gx", "gy"), split_axis=0, concat_axis=0, tiled=True)
    moved = moved.reshape(devices * ROWS, LANES)
    arrived = exchange(call(faces_kernel, FULL.shapes(), 10**6, state), ())
    *speeds, ghosts = call(unpack_kernel, [SPEED, SPEED, GHOSTS], 10**6, moved)
    elec = [(3, SIDE, SIDE, 8, LANES)]

    def finish(coef, form, ghosts, next_form, speed, pre, *arrived):
        def kernel(*refs):
            finish_kernel(
                coef, form, ghosts is not None, next_form, speed is not None, *refs
            )

        extra = [array for array in (ghosts, speed) if array is not None]
        shapes = [STATE] if next_form is None else [STATE, *next_form.shapes()]
        return call(kernel, shapes, 10**6, pre, *arrived, *extra)

    def inner(coef, forms, state, *arrived):
        def kernel(*refs):
            inside_kernel(coef, forms, *refs)

        return call(kernel, INNER, 10**7, state, ghosts, *arrived)

    whole, half = STEP_SIZE, 0.5 * STEP_SIZE
    (pre,) = call(first_volume_kernel, [STATE], 10**7, state, speeds[0], scratch=elec)
    middle, *leaving = finish(whole, FULL, ghosts, SHORT, None, pre, *arrived)
    one = list(arrived)
    two = exchange(leaving)
    two += inner(whole, [FULL], state, *one)
    (pre,) = call(second_volume_kernel, [STATE], 10**7, middle, state, speeds[0], scratch=elec)
    state, *leaving = finish(half, SHORT, ghosts, SHORT, speeds[1], pre, *two)
    three = exchange(leaving)
    three += inner(half, [SHORT, FULL], middle, *two, *one)
    (pre,) = call(first_volume_kernel, [STATE], 10**7, state, speeds[1], scratch=elec)
    middle, *leaving = finish(whole, SHORT, None, FULL, speeds[1], pre, *three)
    four = exchange(leaving)
    (pre,) = call(second_volume_kernel, [STATE], 10**7, middle, state, speeds[1], scratch=elec)
    (state,) = finish(half, FULL, None, None, None, pre, *four)
    return state.reshape(fields.shape)


def solution(mesh):
    return jax.shard_map(
        shards,
        mesh=mesh,
        in_specs=(
            P(None, None, None, "gx", "gy", None),
            P(None, None, None, ("gx", "gy"), None, None),
        ),
        out_specs=P(None, None, None, "gx", "gy", None),
        check_vma=False,
    )
```

```python
import jax
import jax.numpy as jnp
import numpy as np
from jax import lax
from jax.experimental import pallas as pl
from jax.experimental.pallas import tpu as pltpu
from jax.sharding import PartitionSpec as P

STEP_SIZE = 0.025
FLUX_COEF = 3.0
KRYLOV = 4
SIDE = 4
LANES = 128
F32 = jnp.float32
VMEM_LIMIT = 24 * 1024 * 1024


def derivative_table():
    points = np.array([-1.0, -1.0 / np.sqrt(5.0), 1.0 / np.sqrt(5.0), 1.0])
    weights_bary = np.ones(4)
    for first in range(4):
        for second in range(4):
            if first != second:
                weights_bary[first] = weights_bary[first] / (points[first] - points[second])
    table = np.zeros((4, 4))
    for first in range(4):
        for second in range(4):
            if first != second:
                table[first, second] = (
                    weights_bary[second] / weights_bary[first] / (points[first] - points[second])
                )
        table[first, first] = -np.sum(table[first])
    return table.astype(np.float32).astype(np.float64)


TABLE = derivative_table()


def rows():
    return lax.broadcasted_iota(jnp.int32, (8, LANES), 0)


def lanes():
    return lax.broadcasted_iota(jnp.int32, (8, LANES), 1)


def roll_rows(value, shift):
    return pltpu.roll(value, shift % 8, 0)


def roll_lanes(value, shift):
    return pltpu.roll(value, shift % LANES, 1)


def cross(u, b):
    return [
        u[1] * b[2] - u[2] * b[1],
        u[2] * b[0] - u[0] * b[2],
        u[0] * b[1] - u[1] * b[0],
    ]


def plus(direction, b, e):
    if direction == 0:
        return [b[0], b[1] - e[2], b[2] + e[1]]
    if direction == 1:
        return [b[0] + e[2], b[1], b[2] - e[0]]
    return [b[0] - e[1], b[1] + e[0], b[2]]


def minus(direction, b, e):
    if direction == 0:
        return [b[0], b[1] + e[2], b[2] - e[1]]
    if direction == 1:
        return [b[0] - e[2], b[1], b[2] + e[0]]
    return [b[0] + e[1], b[1] - e[0], b[2]]


def speed_at(speed, a, b):
    start = (a * SIDE + b) * 8
    return [speed[i, start : start + 8, :] for i in range(3)]


def third_table(coef):
    node = rows() // 2
    parts = []
    for shift in range(SIDE):
        part = jnp.zeros((8, LANES), F32)
        for p in range(SIDE):
            part = jnp.where(node == p, F32(coef * TABLE[p, (p - shift) % SIDE]), part)
        parts.append(part)
    return parts


def weighted(row, terms):
    total = None
    for q in range(SIDE):
        if row[q] != 0.0:
            part = F32(row[q]) * terms[q]
            total = part if total is None else total + part
    return total


class Weights:
    def __init__(self, coef):
        row, lane = rows(), lanes()
        self.table = coef * TABLE
        self.third = third_table(coef)
        self.jump = F32(FLUX_COEF * coef)
        zero = jnp.zeros((8, LANES), F32)
        self.low = row < 4
        low, high = row < 2, row >= 6
        self.own = jnp.where(low | high, self.jump, zero)
        far = (low & (lane > 0)) | (high & (lane < LANES - 1))
        self.other = jnp.where(far, self.jump, zero)
        self.odd = row % 2 == 1
        self.mid_low = jnp.where(self.odd, self.jump, zero)
        self.mid_high = jnp.where(self.odd, zero, self.jump)

    def along_third(self, value):
        total = self.third[0] * value
        for shift in range(1, SIDE):
            total = total + self.third[shift] * roll_rows(value, 2 * shift)
        return total

    def ends(self, up, down):
        below, above = roll_lanes(roll_rows(up, 2), 1), roll_lanes(roll_rows(down, -2), -1)
        own = up if up is down else jnp.where(self.low, up, down)
        return self.other * jnp.where(self.low, below, above) - self.own * own


def volume(k, state, base, speed, elec, out, weights):
    table, jump = weights.table, weights.jump
    mid_low, mid_high = weights.mid_low, weights.mid_high
    along_third = weights.along_third

    for a in range(SIDE):
        for b in range(SIDE):
            field = [state[k, i, a, b] for i in range(3)]
            parts = cross(speed_at(speed, a, b), field)
            for i in range(3):
                elec[i, a, b] = parts[i]
    for a in range(SIDE):
        for b in range(SIDE):
            e = [elec[i, a, b] for i in range(3)]
            m = [state[k, i, a, b] for i in range(3)]
            total = [
                weighted(table[b], [elec[2, a, q] for q in range(SIDE)]) - along_third(e[1]),
                along_third(e[0]) - weighted(table[a], [elec[2, q, b] for q in range(SIDE)]),
                weighted(table[a], [elec[1, q, b] for q in range(SIDE)])
                - weighted(table[b], [elec[0, a, q] for q in range(SIDE)]),
            ]
            up, down = minus(2, m, e), plus(2, m, e)
            for i in range(3):
                total[i] = total[i] + weights.ends(up[i], down[i])
            if a == 0:
                own = minus(0, m, e)
                total = [t - jump * o for t, o in zip(total, own)]
            if a == SIDE - 1:
                own = plus(0, m, e)
                total = [t - jump * o for t, o in zip(total, own)]
            if b == 0:
                own = minus(1, m, e)
                far_b = [state[k, i, a, SIDE - 1] for i in range(3)]
                far_e = [elec[i, a, SIDE - 1] for i in range(3)]
                far = minus(1, far_b, far_e)
                total = [
                    t - jump * o + mid_low * roll_rows(f, 1)
                    for t, o, f in zip(total, own, far)
                ]
            if b == SIDE - 1:
                own = plus(1, m, e)
                far_b = [state[k, i, a, 0] for i in range(3)]
                far_e = [elec[i, a, 0] for i in range(3)]
                far = plus(1, far_b, far_e)
                total = [
                    t - jump * o + mid_high * roll_rows(f, -1)
                    for t, o, f in zip(total, own, far)
                ]
            start = base(k, a, b)
            for i in range(3):
                out[k, i, a, b] = start[i] + total[i]


def parities():
    return lax.axis_index("gx") % 2 == 1, lax.axis_index("gy") % 2 == 1


def pick(condition, yes, no):
    return jnp.where(condition, yes, no)


def pack_rows(first, second, keep_odd):
    odd = rows() % 2 == 1
    if keep_odd:
        return jnp.where(odd, second, roll_rows(first, -1))
    return jnp.where(odd, roll_rows(second, 1), first)


class Form:
    def __init__(self, short):
        self.short = short
        self.x_count, self.y_count = (10, 5) if short else (12, 6)

    def shapes(self):
        x = (KRYLOV, self.x_count, 8, LANES)
        y = (KRYLOV, self.y_count, 8, LANES)
        return [y if name[0] == "y" else x for name in ORDER]

    def x_slot(self, i, b):
        if not self.short:
            return i * SIDE + b
        if i > 0:
            return (i - 1) * SIDE + b
        return {0: 8, SIDE - 1: 9}.get(b)

    def y_slots(self):
        pairs = [(i, 2 * half, 2 * half + 1) for i in range(3) for half in range(2)]
        if self.short:
            pairs = [p for p in pairs if p[0] != 1] + [(1, 0, SIDE - 1)]
        return pairs


ORDER = ("y_even", "x_odd", "y_odd", "x_even")
FULL, SHORT = Form(False), Form(True)


def send_faces(k, form, state, speed, px, py, y_even, x_odd, y_odd, x_even):
    def traces(direction, sign, a, b):
        m = [state[k, i, a, b] for i in range(3)]
        if speed is None:
            return m
        e = cross(speed_at(speed, a, b), m)
        return plus(direction, m, e) if sign > 0 else minus(direction, m, e)

    for b in range(SIDE):
        high = traces(0, -1, SIDE - 1, b)
        low = traces(0, 1, 0, b)
        for i in range(3):
            slot = form.x_slot(i, b)
            if slot is not None:
                x_even[k, slot] = pick(px, low[i], high[i])
                x_odd[k, slot] = pick(px, high[i], low[i])
    high = [traces(1, -1, a, SIDE - 1) for a in range(SIDE)]
    low = [traces(1, 1, a, 0) for a in range(SIDE)]
    for slot, (i, first, second) in enumerate(form.y_slots()):
        up = pack_rows(high[first][i], high[second][i], True)
        down = pack_rows(low[first][i], low[second][i], False)
        y_even[k, slot] = pick(py, down, up)
        y_odd[k, slot] = pick(py, up, down)


class Arrived:
    def __init__(self, form, faces, inner, px, py):
        self.form, self.inner, self.px, self.py = form, inner, px, py
        self.y_even, self.x_odd, self.y_odd, self.x_even = faces

    def x(self, k, side, i, b):
        slot = self.form.x_slot(i, b)
        if slot is None:
            return self.inner[0][k, side, b - 1]
        even, odd = self.x_even[k, slot], self.x_odd[k, slot]
        return pick(self.px, even, odd) if side == 0 else pick(self.px, odd, even)

    def y(self, k, i, a):
        odd_row = rows() % 2 == 1
        for slot, (comp, first, second) in enumerate(self.form.y_slots()):
            if comp == i and a in (first, second):
                even, odd = self.y_even[k, slot], self.y_odd[k, slot]
                low, high = pick(self.py, even, odd), pick(self.py, odd, even)
                if a == first:
                    return jnp.where(odd_row, roll_rows(high, 1), low)
                return jnp.where(odd_row, high, roll_rows(low, -1))
        return self.inner[1][k, a - 1]


def ghost_at(ghost_speed, place):
    return [ghost_speed[i, place * 8 : place * 8 + 8, :] for i in range(3)]


def receive_faces(k, pre, out, ghost_speed, arrived, coef):
    jump = FLUX_COEF * coef
    odd = rows() % 2 == 1
    zero = jnp.zeros((8, LANES), F32)
    mask_low = jnp.where(odd, zero, F32(jump))
    mask_high = jnp.where(odd, F32(jump), zero)
    turn = jnp.where(odd, F32(1.0), F32(-1.0))
    for b in range(SIDE):
        low = [arrived.x(k, 0, i, b) for i in range(3)]
        high = [arrived.x(k, 1, i, b) for i in range(3)]
        if ghost_speed is not None:
            low = minus(0, low, cross(ghost_at(ghost_speed, b), low))
            high = plus(0, high, cross(ghost_at(ghost_speed, SIDE + b), high))
        for i in range(3):
            out[k, i, 0, b] = pre[k, i, 0, b] + F32(jump) * low[i]
            out[k, i, SIDE - 1, b] = pre[k, i, SIDE - 1, b] + F32(jump) * high[i]
    for a in (1, 2):
        for b in range(SIDE):
            for i in range(3):
                out[k, i, a, b] = pre[k, i, a, b]
    for a in range(SIDE):
        both = [arrived.y(k, i, a) for i in range(3)]
        if ghost_speed is not None:
            e = cross(ghost_at(ghost_speed, 2 * SIDE + a), both)
            both = [both[0] + turn * e[2], both[1], both[2] - turn * e[0]]
        for i in range(3):
            out[k, i, a, 0] = out[k, i, a, 0] + mask_low * both[i]
            out[k, i, a, SIDE - 1] = out[k, i, a, SIDE - 1] + mask_high * both[i]


def inside(k, state, now, before, ghost_speed, inner_x, inner_y, weights):
    table, jump, odd = weights.table, weights.jump, weights.odd
    along_third, ends = weights.along_third, weights.ends
    zero = jnp.zeros((8, LANES), F32)
    at_x, at_y = lax.axis_index("gx"), lax.axis_index("gy")
    last_x, last_y = lax.axis_size("gx") - 1, lax.axis_size("gy") - 1

    def start(value, old):
        return value if old is None else F32(0.5) * (value + old)

    for side in range(2):
        there = at_x > 0 if side == 0 else at_x < last_x
        m = [[now.x(k, side, i, b) for i in range(3)] for b in range(SIDE)]
        e = [cross(ghost_at(ghost_speed, side * SIDE + b), m[b]) for b in range(SIDE)]
        for b in (1, 2):
            own = m[b][0]
            total = weighted(table[b], [e[q][2] for q in range(SIDE)]) - along_third(e[b][1])
            total = total + ends(own + e[b][1], own - e[b][1])
            total = total + jump * (state[k, 0, (SIDE - 1) * side, b] - own)
            old = None if before is None else before.x(k, side, 0, b)
            inner_x[k, side, b - 1] = pick(there, start(own, old) + total, zero)
    m = [[now.y(k, i, a) for i in range(3)] for a in range(SIDE)]
    e = [cross(ghost_at(ghost_speed, 2 * SIDE + a), m[a]) for a in range(SIDE)]
    for a in (1, 2):
        own = m[a][1]
        total = along_third(e[a][0]) - weighted(table[a], [e[q][2] for q in range(SIDE)])
        total = total + ends(own - e[a][0], own + e[a][0])
        mine = jnp.where(odd, state[k, 1, a, SIDE - 1], state[k, 1, a, 0])
        total = total + jump * (mine - own)
        old = None if before is None else before.y(k, 1, a)
        value = start(own, old) + total
        low = pick(at_y > 0, value, zero)
        high = pick(at_y < last_y, value, zero)
        inner_y[k, a - 1] = jnp.where(odd, high, low)


ROWS = 9


def pack_kernel(velocity, out):
    wide = velocity.shape[1]
    pairs = velocity.shape[2] // 2
    lane = lax.broadcasted_iota(jnp.int32, (pairs, 64), 1)
    upper = lane % 16 >= 12

    def both(q, x):
        return [velocity[q, x, pl.ds(j, pairs, stride=2), :] for j in range(2)]

    def store(x, q, value):
        out[pl.ds(x * pairs * ROWS + q, pairs, stride=ROWS), :] = value

    for x in range(wide):
        for q in range(6):
            store(x, q, jnp.concatenate(both(q, x), axis=1))
        for q in range(3):
            even, odd = both(q, x)
            even_low, odd_low = both(q, (x - 1) % wide)
            even_high, odd_high = both(q, (x + 1) % wide)
            y_part = jnp.where(upper, pltpu.roll(odd, 1, 0), pltpu.roll(even, pairs - 1, 0))
            store(
                x,
                6 + q,
                jnp.concatenate(
                    [
                        y_part,
                        even_high[:, :16],
                        odd_high[:, :16],
                        odd_low[:, 48:],
                        even_low[:, 48:],
                    ],
                    axis=1,
                ),
            )


def faces_kernel(state, *faces):
    px, py = parities()

    def step(k, carry):
        send_faces(k, FULL, state, None, px, py, *faces)
        return carry

    lax.fori_loop(0, KRYLOV, step, 0)


def unpack_kernel(arrived, first, second, ghosts):
    for q in range(ROWS):
        block = arrived[pl.ds(q, LANES, stride=ROWS), :].T
        if q < 6:
            into = first if q < 3 else second
            into[q % 3, pl.ds(0, 64, stride=2), :] = block[:64]
            into[q % 3, pl.ds(1, 64, stride=2), :] = block[64:]
        else:
            i = q - 6
            ghosts[i, pl.ds(0, 16, stride=2), :] = block[112:]
            ghosts[i, pl.ds(1, 16, stride=2), :] = block[96:112]
            ghosts[i, pl.ds(32, 16, stride=2), :] = block[64:80]
            ghosts[i, pl.ds(33, 16, stride=2), :] = block[80:96]
            for a in range(SIDE):
                ghosts[i, pl.ds(64 + a * 8, 4, stride=2), :] = block[a * 16 + 12 : a * 16 + 16]
                ghosts[i, pl.ds(65 + a * 8, 4, stride=2), :] = block[a * 16 : a * 16 + 4]


def first_volume_kernel(state, speed, pre, elec):
    weights = Weights(STEP_SIZE)

    def base(k, a, b):
        return [state[k, i, a, b] for i in range(3)]

    def step(k, carry):
        volume(k, state, base, speed, elec, pre, weights)
        return carry

    lax.fori_loop(0, KRYLOV, step, 0, unroll=True)


def second_volume_kernel(state, start, speed, pre, elec):
    weights = Weights(0.5 * STEP_SIZE)

    def base(k, a, b):
        return [F32(0.5) * (state[k, i, a, b] + start[k, i, a, b]) for i in range(3)]

    def step(k, carry):
        volume(k, state, base, speed, elec, pre, weights)
        return carry

    lax.fori_loop(0, KRYLOV, step, 0, unroll=True)


def inside_kernel(coef, forms, *refs):
    px, py = parities()
    state, ghost_speed, *refs, inner_x, inner_y = refs
    stages = []
    for form in forms:
        faces, refs = refs[:4], refs[4:]
        inner = None
        if form.short:
            inner, refs = refs[:2], refs[2:]
        stages.append(Arrived(form, faces, inner, px, py))
    now = stages[0]
    before = stages[1] if len(stages) > 1 else None
    weights = Weights(coef)

    def step(k, carry):
        inside(k, state, now, before, ghost_speed, inner_x, inner_y, weights)
        return carry

    lax.fori_loop(0, KRYLOV, step, 0)


def finish_kernel(coef, form, has_ghosts, next_form, next_speed, *refs):
    px, py = parities()
    pre, *refs = refs
    faces, refs = refs[:4], refs[4:]
    inner = ghosts = speed = None
    if form.short:
        inner, refs = refs[:2], refs[2:]
    if has_ghosts:
        ghosts, *refs = refs
    if next_speed:
        speed, *refs = refs
    out, *leaving = refs
    arrived = Arrived(form, faces, inner, px, py)

    def step(k, carry):
        receive_faces(k, pre, out, ghosts, arrived, coef)
        if next_form is not None:
            send_faces(k, next_form, out, speed, px, py, *leaving)
        return carry

    lax.fori_loop(0, KRYLOV, step, 0)


def last_kernel(coef, pre, *refs):
    *faces, result, out, written = refs
    px, py = parities()
    arrived = Arrived(FULL, faces, None, px, py)

    def copy(k):
        return pltpu.make_async_copy(out.at[k], result.at[k], written.at[k])

    for k in range(KRYLOV):
        receive_faces(k, pre, out, None, arrived, coef)
        copy(k).start()
    for k in range(KRYLOV):
        copy(k).wait()


STATE = (KRYLOV, 3, SIDE, SIDE, 8, LANES)
INNER = [(KRYLOV, 2, 2, 8, LANES), (KRYLOV, 2, 8, LANES)]
SPEED = (3, 128, LANES)
GHOSTS = (3, 96, LANES)


def call(kernel, shapes, flops, *operands, scratch=()):
    whole = pl.BlockSpec(memory_space=pltpu.VMEM)
    return pl.pallas_call(
        kernel,
        out_shape=[jax.ShapeDtypeStruct(shape, F32) for shape in shapes],
        in_specs=[whole] * len(operands),
        out_specs=[whole] * len(shapes),
        scratch_shapes=[pltpu.VMEM(shape, F32) for shape in scratch],
        compiler_params=pltpu.CompilerParams(vmem_limit_bytes=VMEM_LIMIT),
        cost_estimate=pl.CostEstimate(
            flops=flops, bytes_accessed=2 * 1024 * 1024, transcendentals=0
        ),
    )(*operands)


WAITS = (("y_even", 15 * 10**8), ("x_odd", 10**10))


def exchange(faces, waits=WAITS):
    received = []
    for index, face in enumerate(faces):
        axis = "gx" if ORDER[index][0] == "x" else "gy"
        count = lax.axis_size(axis)
        if ORDER[index][2:] == "even":
            pairs = [(i, i ^ 1) for i in range(count)]
        else:
            pairs = [(i, ((i - 1) ^ 1) + 1) for i in range(1, count - 1)]
        received.append(lax.ppermute(face, axis, pairs))
    return in_order(received, waits)


def pass_kernel(arrived, *refs):
    refs[-1][...] = arrived[...]


def in_order(received, waits):
    whole = pl.BlockSpec(memory_space=pltpu.VMEM)
    before = ()
    for name, flops in waits:
        index = ORDER.index(name)
        array = received[index]
        received[index] = pl.pallas_call(
            pass_kernel,
            out_shape=jax.ShapeDtypeStruct(array.shape, F32),
            in_specs=[whole] + [pl.BlockSpec(memory_space=pl.ANY)] * len(before),
            out_specs=whole,
            compiler_params=pltpu.CompilerParams(vmem_limit_bytes=VMEM_LIMIT),
            cost_estimate=pl.CostEstimate(
                flops=flops, bytes_accessed=flops // 100, transcendentals=0
            ),
        )(array, *before)
        before = (received[index],)
    return received


def shards(fields, velocity):
    phases, comps, nodes, slab, wide_x, wide_y = velocity.shape
    devices = lax.axis_size("gx") * lax.axis_size("gy")
    state = fields.reshape(STATE)
    layers = jnp.transpose(velocity, (0, 1, 3, 4, 5, 2))
    layers = layers.reshape(phases * comps, wide_x, wide_y, nodes)
    (packed,) = call(pack_kernel, [(devices * ROWS, LANES)], 10**6, layers)
    packed = packed.reshape(devices, ROWS * LANES)
    moved = lax.all_to_all(packed, ("gx", "gy"), split_axis=0, concat_axis=0, tiled=True)
    moved = moved.reshape(devices * ROWS, LANES)
    arrived = exchange(call(faces_kernel, FULL.shapes(), 10**6, state), ())
    *speeds, ghosts = call(unpack_kernel, [SPEED, SPEED, GHOSTS], 10**6, moved)
    elec = [(3, SIDE, SIDE, 8, LANES)]

    def finish(coef, form, ghosts, next_form, speed, pre, *arrived):
        def kernel(*refs):
            finish_kernel(
                coef, form, ghosts is not None, next_form, speed is not None, *refs
            )

        extra = [array for array in (ghosts, speed) if array is not None]
        shapes = [STATE] if next_form is None else [STATE, *next_form.shapes()]
        return call(kernel, shapes, 10**6, pre, *arrived, *extra)

    def inner(coef, forms, state, *arrived):
        def kernel(*refs):
            inside_kernel(coef, forms, *refs)

        return call(kernel, INNER, 10**7, state, ghosts, *arrived)

    whole, half = STEP_SIZE, 0.5 * STEP_SIZE
    (pre,) = call(first_volume_kernel, [STATE], 10**7, state, speeds[0], scratch=elec)
    middle, *leaving = finish(whole, FULL, ghosts, SHORT, None, pre, *arrived)
    one = list(arrived)
    two = exchange(leaving)
    two += inner(whole, [FULL], state, *one)
    (pre,) = call(second_volume_kernel, [STATE], 10**7, middle, state, speeds[0], scratch=elec)
    state, *leaving = finish(half, SHORT, ghosts, SHORT, speeds[1], pre, *two)
    three = exchange(leaving)
    three += inner(half, [SHORT, FULL], middle, *two, *one)
    (pre,) = call(first_volume_kernel, [STATE], 10**7, state, speeds[1], scratch=elec)
    middle, *leaving = finish(whole, SHORT, None, FULL, speeds[1], pre, *three)
    four = exchange(leaving)
    (pre,) = call(second_volume_kernel, [STATE], 10**7, middle, state, speeds[1], scratch=elec)

    def last(*refs):
        last_kernel(half, *refs)

    state = pl.pallas_call(
        last,
        out_shape=jax.ShapeDtypeStruct(STATE, F32),
        in_specs=[pl.BlockSpec(memory_space=pltpu.VMEM)] * 5,
        out_specs=pl.BlockSpec(memory_space=pltpu.HBM),
        scratch_shapes=[pltpu.VMEM(STATE, F32), pltpu.SemaphoreType.DMA((KRYLOV,))],
        compiler_params=pltpu.CompilerParams(vmem_limit_bytes=VMEM_LIMIT),
        cost_estimate=pl.CostEstimate(flops=10**6, bytes_accessed=2 * 10**6, transcendentals=0),
    )(pre, *four)
    return state.reshape(fields.shape)


def solution(mesh):
    return jax.shard_map(
        shards,
        mesh=mesh,
        in_specs=(
            P(None, None, None, "gx", "gy", None),
            P(None, None, None, ("gx", "gy"), None, None),
        ),
        out_specs=P(None, None, None, "gx", "gy", None),
        check_vma=False,
    )
```

```python
import jax
import jax.numpy as jnp
import numpy as np
from jax import lax
from jax.experimental import pallas as pl
from jax.experimental.pallas import tpu as pltpu
from jax.sharding import PartitionSpec as P

STEP_SIZE = 0.025
FLUX_COEF = 3.0
KRYLOV = 4
SIDE = 4
LANES = 128
F32 = jnp.float32
VMEM_LIMIT = 24 * 1024 * 1024


def derivative_table():
    points = np.array([-1.0, -1.0 / np.sqrt(5.0), 1.0 / np.sqrt(5.0), 1.0])
    weights_bary = np.ones(4)
    for first in range(4):
        for second in range(4):
            if first != second:
                weights_bary[first] = weights_bary[first] / (points[first] - points[second])
    table = np.zeros((4, 4))
    for first in range(4):
        for second in range(4):
            if first != second:
                table[first, second] = (
                    weights_bary[second] / weights_bary[first] / (points[first] - points[second])
                )
        table[first, first] = -np.sum(table[first])
    return table.astype(np.float32).astype(np.float64)


TABLE = derivative_table()


def rows():
    return lax.broadcasted_iota(jnp.int32, (8, LANES), 0)


def lanes():
    return lax.broadcasted_iota(jnp.int32, (8, LANES), 1)


def roll_rows(value, shift):
    return pltpu.roll(value, shift % 8, 0)


def roll_lanes(value, shift):
    return pltpu.roll(value, shift % LANES, 1)


def cross(u, b):
    return [
        u[1] * b[2] - u[2] * b[1],
        u[2] * b[0] - u[0] * b[2],
        u[0] * b[1] - u[1] * b[0],
    ]


def plus(direction, b, e):
    if direction == 0:
        return [b[0], b[1] - e[2], b[2] + e[1]]
    if direction == 1:
        return [b[0] + e[2], b[1], b[2] - e[0]]
    return [b[0] - e[1], b[1] + e[0], b[2]]


def minus(direction, b, e):
    if direction == 0:
        return [b[0], b[1] + e[2], b[2] - e[1]]
    if direction == 1:
        return [b[0] - e[2], b[1], b[2] + e[0]]
    return [b[0] + e[1], b[1] - e[0], b[2]]


def speed_at(speed, a, b):
    start = (a * SIDE + b) * 8
    return [speed[i, start : start + 8, :] for i in range(3)]


def third_table(coef):
    node = rows() // 2
    parts = []
    for shift in range(SIDE):
        part = jnp.zeros((8, LANES), F32)
        for p in range(SIDE):
            part = jnp.where(node == p, F32(coef * TABLE[p, (p - shift) % SIDE]), part)
        parts.append(part)
    return parts


def weighted(row, terms):
    total = None
    for q in range(SIDE):
        if row[q] != 0.0:
            part = F32(row[q]) * terms[q]
            total = part if total is None else total + part
    return total


def volume(k, state, base, speed, elec, out, coef):
    row, lane = rows(), lanes()
    table = coef * TABLE
    third = third_table(coef)
    jump = FLUX_COEF * coef
    zero = jnp.zeros((8, LANES), F32)
    own_low = jnp.where(row < 2, F32(jump), zero)
    own_high = jnp.where(row >= 6, F32(jump), zero)
    in_low = jnp.where(lane > 0, own_low, zero)
    in_high = jnp.where(lane < LANES - 1, own_high, zero)
    odd = row % 2 == 1
    mid_low = jnp.where(odd, F32(jump), zero)
    mid_high = jnp.where(odd, zero, F32(jump))

    def along_third(value):
        total = third[0] * value
        for shift in range(1, SIDE):
            total = total + third[shift] * roll_rows(value, 2 * shift)
        return total

    for a in range(SIDE):
        for b in range(SIDE):
            field = [state[k, i, a, b] for i in range(3)]
            parts = cross(speed_at(speed, a, b), field)
            for i in range(3):
                elec[i, a, b] = parts[i]
    for a in range(SIDE):
        for b in range(SIDE):
            e = [elec[i, a, b] for i in range(3)]
            m = [state[k, i, a, b] for i in range(3)]
            total = [
                weighted(table[b], [elec[2, a, q] for q in range(SIDE)]) - along_third(e[1]),
                along_third(e[0]) - weighted(table[a], [elec[2, q, b] for q in range(SIDE)]),
                weighted(table[a], [elec[1, q, b] for q in range(SIDE)])
                - weighted(table[b], [elec[0, a, q] for q in range(SIDE)]),
            ]
            up, down = minus(2, m, e), plus(2, m, e)
            for i in range(3):
                total[i] = total[i] - (own_low * up[i] + own_high * down[i])
                total[i] = total[i] + in_low * roll_lanes(roll_rows(up[i], 2), 1)
                total[i] = total[i] + in_high * roll_lanes(roll_rows(down[i], -2), -1)
            if a == 0:
                own = minus(0, m, e)
                total = [t - F32(jump) * o for t, o in zip(total, own)]
            if a == SIDE - 1:
                own = plus(0, m, e)
                total = [t - F32(jump) * o for t, o in zip(total, own)]
            if b == 0:
                own = minus(1, m, e)
                far_b = [state[k, i, a, SIDE - 1] for i in range(3)]
                far_e = [elec[i, a, SIDE - 1] for i in range(3)]
                far = minus(1, far_b, far_e)
                total = [
                    t - F32(jump) * o + mid_low * roll_rows(f, 1)
                    for t, o, f in zip(total, own, far)
                ]
            if b == SIDE - 1:
                own = plus(1, m, e)
                far_b = [state[k, i, a, 0] for i in range(3)]
                far_e = [elec[i, a, 0] for i in range(3)]
                far = plus(1, far_b, far_e)
                total = [
                    t - F32(jump) * o + mid_high * roll_rows(f, -1)
                    for t, o, f in zip(total, own, far)
                ]
            start = base(k, a, b)
            for i in range(3):
                out[k, i, a, b] = start[i] + total[i]


def parities():
    return lax.axis_index("gx") % 2 == 1, lax.axis_index("gy") % 2 == 1


def pick(condition, yes, no):
    return jnp.where(condition, yes, no)


def pack_rows(first, second, keep_odd):
    odd = rows() % 2 == 1
    if keep_odd:
        return jnp.where(odd, second, roll_rows(first, -1))
    return jnp.where(odd, roll_rows(second, 1), first)


class Form:
    def __init__(self, short):
        self.short = short
        self.x_count, self.y_count = (10, 5) if short else (12, 6)

    def shapes(self):
        x = (KRYLOV, self.x_count, 8, LANES)
        y = (KRYLOV, self.y_count, 8, LANES)
        return [y if name[0] == "y" else x for name in ORDER]

    def x_slot(self, i, b):
        if not self.short:
            return i * SIDE + b
        if i > 0:
            return (i - 1) * SIDE + b
        return {0: 8, SIDE - 1: 9}.get(b)

    def y_slots(self):
        pairs = [(i, 2 * half, 2 * half + 1) for i in range(3) for half in range(2)]
        if self.short:
            pairs = [p for p in pairs if p[0] != 1] + [(1, 0, SIDE - 1)]
        return pairs


ORDER = ("y_even", "x_odd", "y_odd", "x_even")
FULL, SHORT = Form(False), Form(True)


def send_faces(k, form, state, speed, px, py, y_even, x_odd, y_odd, x_even):
    def traces(direction, sign, a, b):
        m = [state[k, i, a, b] for i in range(3)]
        if speed is None:
            return m
        e = cross(speed_at(speed, a, b), m)
        return plus(direction, m, e) if sign > 0 else minus(direction, m, e)

    for b in range(SIDE):
        high = traces(0, -1, SIDE - 1, b)
        low = traces(0, 1, 0, b)
        for i in range(3):
            slot = form.x_slot(i, b)
            if slot is not None:
                x_even[k, slot] = pick(px, low[i], high[i])
                x_odd[k, slot] = pick(px, high[i], low[i])
    high = [traces(1, -1, a, SIDE - 1) for a in range(SIDE)]
    low = [traces(1, 1, a, 0) for a in range(SIDE)]
    for slot, (i, first, second) in enumerate(form.y_slots()):
        up = pack_rows(high[first][i], high[second][i], True)
        down = pack_rows(low[first][i], low[second][i], False)
        y_even[k, slot] = pick(py, down, up)
        y_odd[k, slot] = pick(py, up, down)


class Ghosts:
    def __init__(self, here, partner, px):
        self.here, self.partner, self.px = here, partner, px

    def x(self, side, b):
        part = pl.ds(b * 8, 8)
        values = []
        for i in range(3):
            even, odd = self.partner[i, part, :], self.here[i, part, :]
            values.append(pick(self.px, even, odd) if side == 0 else pick(self.px, odd, even))
        return values

    def y(self, a):
        start = (SIDE + a) * 8
        return [self.here[i, start : start + 8, :] for i in range(3)]


class Arrived:
    def __init__(self, form, faces, inner, px, py):
        self.form, self.inner, self.px, self.py = form, inner, px, py
        self.y_even, self.x_odd, self.y_odd, self.x_even = faces

    def x(self, k, side, i, b):
        slot = self.form.x_slot(i, b)
        if slot is None:
            return self.inner[0][k, side, b - 1]
        even, odd = self.x_even[k, slot], self.x_odd[k, slot]
        return pick(self.px, even, odd) if side == 0 else pick(self.px, odd, even)

    def y(self, k, i, a):
        odd_row = rows() % 2 == 1
        for slot, (comp, first, second) in enumerate(self.form.y_slots()):
            if comp == i and a in (first, second):
                even, odd = self.y_even[k, slot], self.y_odd[k, slot]
                low, high = pick(self.py, even, odd), pick(self.py, odd, even)
                if a == first:
                    return jnp.where(odd_row, roll_rows(high, 1), low)
                return jnp.where(odd_row, high, roll_rows(low, -1))
        return self.inner[1][k, a - 1]


def receive_faces(k, pre, out, ghosts, arrived, coef):
    jump = FLUX_COEF * coef
    odd = rows() % 2 == 1
    zero = jnp.zeros((8, LANES), F32)
    mask_low = jnp.where(odd, zero, F32(jump))
    mask_high = jnp.where(odd, F32(jump), zero)
    turn = jnp.where(odd, F32(1.0), F32(-1.0))
    for b in range(SIDE):
        low = [arrived.x(k, 0, i, b) for i in range(3)]
        high = [arrived.x(k, 1, i, b) for i in range(3)]
        if ghosts is not None:
            low = minus(0, low, cross(ghosts.x(0, b), low))
            high = plus(0, high, cross(ghosts.x(1, b), high))
        for i in range(3):
            out[k, i, 0, b] = pre[k, i, 0, b] + F32(jump) * low[i]
            out[k, i, SIDE - 1, b] = pre[k, i, SIDE - 1, b] + F32(jump) * high[i]
    for a in (1, 2):
        for b in range(SIDE):
            for i in range(3):
                out[k, i, a, b] = pre[k, i, a, b]
    for a in range(SIDE):
        both = [arrived.y(k, i, a) for i in range(3)]
        if ghosts is not None:
            e = cross(ghosts.y(a), both)
            both = [both[0] + turn * e[2], both[1], both[2] - turn * e[0]]
        for i in range(3):
            out[k, i, a, 0] = out[k, i, a, 0] + mask_low * both[i]
            out[k, i, a, SIDE - 1] = out[k, i, a, SIDE - 1] + mask_high * both[i]


def inside(k, state, now, before, ghosts, inner_x, inner_y, coef):
    row, lane = rows(), lanes()
    table = coef * TABLE
    third = third_table(coef)
    jump = FLUX_COEF * coef
    zero = jnp.zeros((8, LANES), F32)
    own_low = jnp.where(row < 2, F32(jump), zero)
    own_high = jnp.where(row >= 6, F32(jump), zero)
    in_low = jnp.where(lane > 0, own_low, zero)
    in_high = jnp.where(lane < LANES - 1, own_high, zero)
    odd = row % 2 == 1
    at_x, at_y = lax.axis_index("gx"), lax.axis_index("gy")
    last_x, last_y = lax.axis_size("gx") - 1, lax.axis_size("gy") - 1

    def along_third(value):
        total = third[0] * value
        for shift in range(1, SIDE):
            total = total + third[shift] * roll_rows(value, 2 * shift)
        return total

    def ends(up, down):
        total = in_low * roll_lanes(roll_rows(up, 2), 1) - own_low * up
        return total + in_high * roll_lanes(roll_rows(down, -2), -1) - own_high * down

    def start(value, old):
        return value if old is None else F32(0.5) * (value + old)

    for side in range(2):
        there = at_x > 0 if side == 0 else at_x < last_x
        m = [[now.x(k, side, i, b) for i in range(3)] for b in range(SIDE)]
        e = [cross(ghosts.x(side, b), m[b]) for b in range(SIDE)]
        for b in (1, 2):
            own = m[b][0]
            total = weighted(table[b], [e[q][2] for q in range(SIDE)]) - along_third(e[b][1])
            total = total + ends(own + e[b][1], own - e[b][1])
            total = total + F32(jump) * (state[k, 0, (SIDE - 1) * side, b] - own)
            old = None if before is None else before.x(k, side, 0, b)
            inner_x[k, side, b - 1] = pick(there, start(own, old) + total, zero)
    m = [[now.y(k, i, a) for i in range(3)] for a in range(SIDE)]
    e = [cross(ghosts.y(a), m[a]) for a in range(SIDE)]
    for a in (1, 2):
        own = m[a][1]
        total = along_third(e[a][0]) - weighted(table[a], [e[q][2] for q in range(SIDE)])
        total = total + ends(own - e[a][0], own + e[a][0])
        mine = jnp.where(odd, state[k, 1, a, SIDE - 1], state[k, 1, a, 0])
        total = total + F32(jump) * (mine - own)
        old = None if before is None else before.y(k, 1, a)
        value = start(own, old) + total
        low = pick(at_y > 0, value, zero)
        high = pick(at_y < last_y, value, zero)
        inner_y[k, a - 1] = jnp.where(odd, high, low)


ROWS = 8


def pack_kernel(velocity, out):
    wide = velocity.shape[1]
    pairs = velocity.shape[2] // 2
    upper = lax.broadcasted_iota(jnp.int32, (pairs, 64), 1) % 16 >= 12
    lane = lax.broadcasted_iota(jnp.int32, (pairs, LANES), 1)
    inner = (lane % 16 >= 4) & (lane % 16 < 12)

    def both(q, x):
        return [velocity[q, x, pl.ds(j, pairs, stride=2), :] for j in range(2)]

    def store(x, q, value):
        out[pl.ds(x * pairs * ROWS + q, pairs, stride=ROWS), :] = value

    for x in range(wide):
        for q in range(6):
            store(x, q, jnp.concatenate(both(q, x), axis=1))
        beside, nodes = (max(x - 1, 0), 48) if x % 2 == 0 else (min(x + 1, wide - 1), 0)
        y_part = []
        for q in range(3):
            even, odd = both(q, x)
            y_part.append(jnp.where(upper, pltpu.roll(odd, 1, 0), pltpu.roll(even, pairs - 1, 0)))
        third = jnp.concatenate(both(2, beside), axis=1)
        row = jnp.concatenate(y_part[:2], axis=1)
        row = jnp.where(inner, pltpu.roll(third, 24, 1), row)
        row = jnp.where(inner & (lane % 64 // 16 == nodes // 16), third, row)
        store(x, 6, row)
        pieces = [v[:, nodes : nodes + 16] for q in range(2) for v in both(q, beside)]
        store(x, 7, jnp.concatenate([y_part[2], *pieces], axis=1))


def faces_kernel(state, *faces):
    px, py = parities()

    def step(k, carry):
        send_faces(k, FULL, state, None, px, py, *faces)
        return carry

    lax.fori_loop(0, KRYLOV, step, 0)


def unpack_kernel(arrived, first, second, here, partner):
    px, _ = parities()
    blocks = [arrived[pl.ds(q, LANES, stride=ROWS), :].T for q in range(ROWS)]
    for q in range(6):
        into = first if q < 3 else second
        into[q % 3, pl.ds(0, 64, stride=2), :] = blocks[q][:64]
        into[q % 3, pl.ds(1, 64, stride=2), :] = blocks[q][64:]
    for i in range(3):
        block = blocks[6][64 * i : 64 * i + 64] if i < 2 else blocks[7][:64]
        for a in range(SIDE):
            low, high = block[a * 16 + 12 : a * 16 + 16], block[a * 16 : a * 16 + 4]
            here[i, pl.ds(32 + a * 8, 4, stride=2), :] = low
            here[i, pl.ds(33 + a * 8, 4, stride=2), :] = high
    for i in range(2):
        for j in range(2):
            start = 64 + 32 * i + 16 * j
            here[i, pl.ds(j, 16, stride=2), :] = blocks[7][start : start + 16]
    for j in range(2):
        for b in range(SIDE):
            shift = 4 * b if b in (1, 2) else 4 * b + 24
            places = [(group * 16 + 64 * j + shift) % LANES for group in (3, 0)]
            low, high = [blocks[6][place : place + 4] for place in places]
            here[2, pl.ds(b * 8 + j, 4, stride=2), :] = pick(px, high, low)
    for i in range(3):
        for b in range(SIDE):
            low = first[i, b * 8 : b * 8 + 8, :]
            high = first[i, 96 + b * 8 : 104 + b * 8, :]
            partner[i, b * 8 : b * 8 + 8, :] = pick(px, low, high)


def first_volume_kernel(state, speed, pre, elec):
    def base(k, a, b):
        return [state[k, i, a, b] for i in range(3)]

    def step(k, carry):
        volume(k, state, base, speed, elec, pre, STEP_SIZE)
        return carry

    lax.fori_loop(0, KRYLOV, step, 0)


def second_volume_kernel(state, start, speed, pre, elec):
    def base(k, a, b):
        return [F32(0.5) * (state[k, i, a, b] + start[k, i, a, b]) for i in range(3)]

    def step(k, carry):
        volume(k, state, base, speed, elec, pre, 0.5 * STEP_SIZE)
        return carry

    lax.fori_loop(0, KRYLOV, step, 0)


def inside_kernel(coef, forms, *refs):
    px, py = parities()
    state, here, partner, *refs, inner_x, inner_y = refs
    ghosts = Ghosts(here, partner, px)
    stages = []
    for form in forms:
        faces, refs = refs[:4], refs[4:]
        inner = None
        if form.short:
            inner, refs = refs[:2], refs[2:]
        stages.append(Arrived(form, faces, inner, px, py))
    now = stages[0]
    before = stages[1] if len(stages) > 1 else None

    def step(k, carry):
        inside(k, state, now, before, ghosts, inner_x, inner_y, coef)
        return carry

    lax.fori_loop(0, KRYLOV, step, 0)


def finish_kernel(coef, form, has_ghosts, next_form, next_speed, *refs):
    px, py = parities()
    pre, *refs = refs
    faces, refs = refs[:4], refs[4:]
    inner = ghosts = speed = None
    if form.short:
        inner, refs = refs[:2], refs[2:]
    if has_ghosts:
        here, partner, *refs = refs
        ghosts = Ghosts(here, partner, px)
    if next_speed:
        speed, *refs = refs
    out, *leaving = refs
    arrived = Arrived(form, faces, inner, px, py)

    def step(k, carry):
        receive_faces(k, pre, out, ghosts, arrived, coef)
        if next_form is not None:
            send_faces(k, next_form, out, speed, px, py, *leaving)
        return carry

    lax.fori_loop(0, KRYLOV, step, 0)


STATE = (KRYLOV, 3, SIDE, SIDE, 8, LANES)
INNER = [(KRYLOV, 2, 2, 8, LANES), (KRYLOV, 2, 8, LANES)]
SPEED = (3, 128, LANES)
GHOSTS = (3, 64, LANES)
PARTNER = (3, 32, LANES)


def call(kernel, shapes, flops, *operands, scratch=()):
    whole = pl.BlockSpec(memory_space=pltpu.VMEM)
    return pl.pallas_call(
        kernel,
        out_shape=[jax.ShapeDtypeStruct(shape, F32) for shape in shapes],
        in_specs=[whole] * len(operands),
        out_specs=[whole] * len(shapes),
        scratch_shapes=[pltpu.VMEM(shape, F32) for shape in scratch],
        compiler_params=pltpu.CompilerParams(vmem_limit_bytes=VMEM_LIMIT),
        cost_estimate=pl.CostEstimate(
            flops=flops, bytes_accessed=2 * 1024 * 1024, transcendentals=0
        ),
    )(*operands)


WAITS = (("y_even", 15 * 10**8), ("x_odd", 10**10))


def exchange(faces, waits=WAITS):
    received = []
    for index, face in enumerate(faces):
        axis = "gx" if ORDER[index][0] == "x" else "gy"
        count = lax.axis_size(axis)
        if ORDER[index][2:] == "even":
            pairs = [(i, i ^ 1) for i in range(count)]
        else:
            pairs = [(i, ((i - 1) ^ 1) + 1) for i in range(1, count - 1)]
        received.append(lax.ppermute(face, axis, pairs))
    return in_order(received, waits)


def pass_kernel(arrived, *refs):
    refs[-1][...] = arrived[...]


def in_order(received, waits):
    whole = pl.BlockSpec(memory_space=pltpu.VMEM)
    before = ()
    for name, flops in waits:
        index = ORDER.index(name)
        array = received[index]
        received[index] = pl.pallas_call(
            pass_kernel,
            out_shape=jax.ShapeDtypeStruct(array.shape, F32),
            in_specs=[whole] + [pl.BlockSpec(memory_space=pl.ANY)] * len(before),
            out_specs=whole,
            compiler_params=pltpu.CompilerParams(vmem_limit_bytes=VMEM_LIMIT),
            cost_estimate=pl.CostEstimate(
                flops=flops, bytes_accessed=flops // 100, transcendentals=0
            ),
        )(array, *before)
        before = (received[index],)
    return received


def shards(fields, velocity):
    phases, comps, nodes, slab, wide_x, wide_y = velocity.shape
    devices = lax.axis_size("gx") * lax.axis_size("gy")
    state = fields.reshape(STATE)
    layers = jnp.transpose(velocity, (0, 1, 3, 4, 5, 2))
    layers = layers.reshape(phases * comps, wide_x, wide_y, nodes)
    (packed,) = call(pack_kernel, [(devices * ROWS, LANES)], 10**6, layers)
    packed = packed.reshape(devices, ROWS * LANES)
    moved = lax.all_to_all(packed, ("gx", "gy"), split_axis=0, concat_axis=0, tiled=True)
    moved = moved.reshape(devices * ROWS, LANES)
    arrived = exchange(call(faces_kernel, FULL.shapes(), 10**6, state), ())
    shapes = [SPEED, SPEED, GHOSTS, PARTNER]
    *speeds, here, leaving = call(unpack_kernel, shapes, 10**6, moved)
    count = lax.axis_size("gx")
    partner = lax.ppermute(leaving, "gx", [(i, i ^ 1) for i in range(count)])
    ghosts = (here, partner)
    elec = [(3, SIDE, SIDE, 8, LANES)]

    def finish(coef, form, ghosts, next_form, speed, pre, *arrived):
        def kernel(*refs):
            finish_kernel(
                coef, form, ghosts is not None, next_form, speed is not None, *refs
            )

        extra = [] if ghosts is None else [*ghosts]
        extra += [] if speed is None else [speed]
        shapes = [STATE] if next_form is None else [STATE, *next_form.shapes()]
        return call(kernel, shapes, 10**6, pre, *arrived, *extra)

    def inner(coef, forms, state, *arrived):
        def kernel(*refs):
            inside_kernel(coef, forms, *refs)

        return call(kernel, INNER, 10**7, state, *ghosts, *arrived)

    whole, half = STEP_SIZE, 0.5 * STEP_SIZE
    (pre,) = call(first_volume_kernel, [STATE], 10**7, state, speeds[0], scratch=elec)
    middle, *leaving = finish(whole, FULL, ghosts, SHORT, None, pre, *arrived)
    one = list(arrived)
    two = exchange(leaving)
    two += inner(whole, [FULL], state, *one)
    (pre,) = call(second_volume_kernel, [STATE], 10**7, middle, state, speeds[0], scratch=elec)
    state, *leaving = finish(half, SHORT, ghosts, SHORT, speeds[1], pre, *two)
    three = exchange(leaving)
    three += inner(half, [SHORT, FULL], middle, *two, *one)
    (pre,) = call(first_volume_kernel, [STATE], 10**7, state, speeds[1], scratch=elec)
    middle, *leaving = finish(whole, SHORT, None, FULL, speeds[1], pre, *three)
    four = exchange(leaving)
    (pre,) = call(second_volume_kernel, [STATE], 10**7, middle, state, speeds[1], scratch=elec)
    (state,) = finish(half, FULL, None, None, None, pre, *four)
    return state.reshape(fields.shape)


def solution(mesh):
    return jax.shard_map(
        shards,
        mesh=mesh,
        in_specs=(
            P(None, None, None, "gx", "gy", None),
            P(None, None, None, ("gx", "gy"), None, None),
        ),
        out_specs=P(None, None, None, "gx", "gy", None),
        check_vma=False,
    )
```

```python
import jax
import jax.numpy as jnp
import numpy as np
from jax import lax
from jax.experimental import pallas as pl
from jax.experimental.pallas import tpu as pltpu
from jax.sharding import PartitionSpec as P

STEP_SIZE = 0.025
FLUX_COEF = 3.0
KRYLOV = 4
SIDE = 4
LANES = 128
F32 = jnp.float32
VMEM_LIMIT = 24 * 1024 * 1024


def derivative_table():
    points = np.array([-1.0, -1.0 / np.sqrt(5.0), 1.0 / np.sqrt(5.0), 1.0])
    weights_bary = np.ones(4)
    for first in range(4):
        for second in range(4):
            if first != second:
                weights_bary[first] = weights_bary[first] / (points[first] - points[second])
    table = np.zeros((4, 4))
    for first in range(4):
        for second in range(4):
            if first != second:
                table[first, second] = (
                    weights_bary[second] / weights_bary[first] / (points[first] - points[second])
                )
        table[first, first] = -np.sum(table[first])
    return table.astype(np.float32).astype(np.float64)


TABLE = derivative_table()


def rows():
    return lax.broadcasted_iota(jnp.int32, (8, LANES), 0)


def lanes():
    return lax.broadcasted_iota(jnp.int32, (8, LANES), 1)


def roll_rows(value, shift):
    return pltpu.roll(value, shift % 8, 0)


def roll_lanes(value, shift):
    return pltpu.roll(value, shift % LANES, 1)


def cross(u, b):
    return [
        u[1] * b[2] - u[2] * b[1],
        u[2] * b[0] - u[0] * b[2],
        u[0] * b[1] - u[1] * b[0],
    ]


def plus(direction, b, e):
    if direction == 0:
        return [b[0], b[1] - e[2], b[2] + e[1]]
    if direction == 1:
        return [b[0] + e[2], b[1], b[2] - e[0]]
    return [b[0] - e[1], b[1] + e[0], b[2]]


def minus(direction, b, e):
    if direction == 0:
        return [b[0], b[1] + e[2], b[2] - e[1]]
    if direction == 1:
        return [b[0] - e[2], b[1], b[2] + e[0]]
    return [b[0] + e[1], b[1] - e[0], b[2]]


def speed_at(speed, a, b):
    start = (a * SIDE + b) * 8
    return [speed[i, start : start + 8, :] for i in range(3)]


def third_table(coef):
    node = rows() // 2
    parts = []
    for shift in range(SIDE):
        part = jnp.zeros((8, LANES), F32)
        for p in range(SIDE):
            part = jnp.where(node == p, F32(coef * TABLE[p, (p - shift) % SIDE]), part)
        parts.append(part)
    return parts


def weighted(row, terms):
    total = None
    for q in range(SIDE):
        if row[q] != 0.0:
            part = F32(row[q]) * terms[q]
            total = part if total is None else total + part
    return total


def volume(k, state, base, speed, elec, out, coef):
    row, lane = rows(), lanes()
    table = coef * TABLE
    third = third_table(coef)
    jump = FLUX_COEF * coef
    zero = jnp.zeros((8, LANES), F32)
    own_low = jnp.where(row < 2, F32(jump), zero)
    own_high = jnp.where(row >= 6, F32(jump), zero)
    in_low = jnp.where(lane > 0, own_low, zero)
    in_high = jnp.where(lane < LANES - 1, own_high, zero)
    odd = row % 2 == 1
    mid_low = jnp.where(odd, F32(jump), zero)
    mid_high = jnp.where(odd, zero, F32(jump))

    def along_third(value):
        total = third[0] * value
        for shift in range(1, SIDE):
            total = total + third[shift] * roll_rows(value, 2 * shift)
        return total

    for a in range(SIDE):
        for b in range(SIDE):
            field = [state[k, i, a, b] for i in range(3)]
            parts = cross(speed_at(speed, a, b), field)
            for i in range(3):
                elec[i, a, b] = parts[i]
    for a in range(SIDE):
        for b in range(SIDE):
            e = [elec[i, a, b] for i in range(3)]
            m = [state[k, i, a, b] for i in range(3)]
            total = [
                weighted(table[b], [elec[2, a, q] for q in range(SIDE)]) - along_third(e[1]),
                along_third(e[0]) - weighted(table[a], [elec[2, q, b] for q in range(SIDE)]),
                weighted(table[a], [elec[1, q, b] for q in range(SIDE)])
                - weighted(table[b], [elec[0, a, q] for q in range(SIDE)]),
            ]
            up, down = minus(2, m, e), plus(2, m, e)
            for i in range(3):
                total[i] = total[i] - (own_low * up[i] + own_high * down[i])
                total[i] = total[i] + in_low * roll_lanes(roll_rows(up[i], 2), 1)
                total[i] = total[i] + in_high * roll_lanes(roll_rows(down[i], -2), -1)
            if a == 0:
                own = minus(0, m, e)
                total = [t - F32(jump) * o for t, o in zip(total, own)]
            if a == SIDE - 1:
                own = plus(0, m, e)
                total = [t - F32(jump) * o for t, o in zip(total, own)]
            if b == 0:
                own = minus(1, m, e)
                far_b = [state[k, i, a, SIDE - 1] for i in range(3)]
                far_e = [elec[i, a, SIDE - 1] for i in range(3)]
                far = minus(1, far_b, far_e)
                total = [
                    t - F32(jump) * o + mid_low * roll_rows(f, 1)
                    for t, o, f in zip(total, own, far)
                ]
            if b == SIDE - 1:
                own = plus(1, m, e)
                far_b = [state[k, i, a, 0] for i in range(3)]
                far_e = [elec[i, a, 0] for i in range(3)]
                far = plus(1, far_b, far_e)
                total = [
                    t - F32(jump) * o + mid_high * roll_rows(f, -1)
                    for t, o, f in zip(total, own, far)
                ]
            start = base(k, a, b)
            for i in range(3):
                out[k, i, a, b] = start[i] + total[i]


def parities():
    return lax.axis_index("gx") % 2 == 1, lax.axis_index("gy") % 2 == 1


def pick(condition, yes, no):
    return jnp.where(condition, yes, no)


def pack_rows(first, second, keep_odd):
    odd = rows() % 2 == 1
    if keep_odd:
        return jnp.where(odd, second, roll_rows(first, -1))
    return jnp.where(odd, roll_rows(second, 1), first)


class Form:
    def __init__(self, short):
        self.short = short
        self.x_count, self.y_count = (10, 5) if short else (12, 6)

    def shapes(self):
        x = (KRYLOV, self.x_count, 8, LANES)
        y = (KRYLOV, self.y_count, 8, LANES)
        return [y if name[0] == "y" else x for name in ORDER]

    def x_slot(self, i, b):
        if not self.short:
            return i * SIDE + b
        if i > 0:
            return (i - 1) * SIDE + b
        return {0: 8, SIDE - 1: 9}.get(b)

    def y_slots(self):
        pairs = [(i, 2 * half, 2 * half + 1) for i in range(3) for half in range(2)]
        if self.short:
            pairs = [p for p in pairs if p[0] != 1] + [(1, 0, SIDE - 1)]
        return pairs


ORDER = ("y_even", "x_odd", "y_odd", "x_even")
FULL, SHORT = Form(False), Form(True)


def send_faces(k, form, state, speed, px, py, y_even, x_odd, y_odd, x_even):
    def traces(direction, sign, a, b):
        m = [state[k, i, a, b] for i in range(3)]
        if speed is None:
            return m
        e = cross(speed_at(speed, a, b), m)
        return plus(direction, m, e) if sign > 0 else minus(direction, m, e)

    for b in range(SIDE):
        high = traces(0, -1, SIDE - 1, b)
        low = traces(0, 1, 0, b)
        for i in range(3):
            slot = form.x_slot(i, b)
            if slot is not None:
                x_even[k, slot] = pick(px, low[i], high[i])
                x_odd[k, slot] = pick(px, high[i], low[i])
    high = [traces(1, -1, a, SIDE - 1) for a in range(SIDE)]
    low = [traces(1, 1, a, 0) for a in range(SIDE)]
    for slot, (i, first, second) in enumerate(form.y_slots()):
        up = pack_rows(high[first][i], high[second][i], True)
        down = pack_rows(low[first][i], low[second][i], False)
        y_even[k, slot] = pick(py, down, up)
        y_odd[k, slot] = pick(py, up, down)


class Arrived:
    def __init__(self, form, faces, inner, px, py):
        self.form, self.inner, self.px, self.py = form, inner, px, py
        self.y_even, self.x_odd, self.y_odd, self.x_even = faces

    def x(self, k, side, i, b):
        slot = self.form.x_slot(i, b)
        if slot is None:
            return self.inner[0][k, side, b - 1]
        even, odd = self.x_even[k, slot], self.x_odd[k, slot]
        return pick(self.px, even, odd) if side == 0 else pick(self.px, odd, even)

    def y(self, k, i, a):
        odd_row = rows() % 2 == 1
        for slot, (comp, first, second) in enumerate(self.form.y_slots()):
            if comp == i and a in (first, second):
                even, odd = self.y_even[k, slot], self.y_odd[k, slot]
                low, high = pick(self.py, even, odd), pick(self.py, odd, even)
                if a == first:
                    return jnp.where(odd_row, roll_rows(high, 1), low)
                return jnp.where(odd_row, high, roll_rows(low, -1))
        return self.inner[1][k, a - 1]


def ghost_at(ghost_speed, place):
    return [ghost_speed[i, place * 8 : place * 8 + 8, :] for i in range(3)]


def receive_faces(k, pre, out, ghost_speed, arrived, coef):
    jump = FLUX_COEF * coef
    odd = rows() % 2 == 1
    zero = jnp.zeros((8, LANES), F32)
    mask_low = jnp.where(odd, zero, F32(jump))
    mask_high = jnp.where(odd, F32(jump), zero)
    turn = jnp.where(odd, F32(1.0), F32(-1.0))
    for b in range(SIDE):
        low = [arrived.x(k, 0, i, b) for i in range(3)]
        high = [arrived.x(k, 1, i, b) for i in range(3)]
        if ghost_speed is not None:
            low = minus(0, low, cross(ghost_at(ghost_speed, b), low))
            high = plus(0, high, cross(ghost_at(ghost_speed, SIDE + b), high))
        for i in range(3):
            out[k, i, 0, b] = pre[k, i, 0, b] + F32(jump) * low[i]
            out[k, i, SIDE - 1, b] = pre[k, i, SIDE - 1, b] + F32(jump) * high[i]
    for a in (1, 2):
        for b in range(SIDE):
            for i in range(3):
                out[k, i, a, b] = pre[k, i, a, b]
    for a in range(SIDE):
        both = [arrived.y(k, i, a) for i in range(3)]
        if ghost_speed is not None:
            e = cross(ghost_at(ghost_speed, 2 * SIDE + a), both)
            both = [both[0] + turn * e[2], both[1], both[2] - turn * e[0]]
        for i in range(3):
            out[k, i, a, 0] = out[k, i, a, 0] + mask_low * both[i]
            out[k, i, a, SIDE - 1] = out[k, i, a, SIDE - 1] + mask_high * both[i]


def inside(k, state, now, before, ghost_speed, inner_x, inner_y, coef):
    row, lane = rows(), lanes()
    table = coef * TABLE
    third = third_table(coef)
    jump = FLUX_COEF * coef
    zero = jnp.zeros((8, LANES), F32)
    own_low = jnp.where(row < 2, F32(jump), zero)
    own_high = jnp.where(row >= 6, F32(jump), zero)
    in_low = jnp.where(lane > 0, own_low, zero)
    in_high = jnp.where(lane < LANES - 1, own_high, zero)
    odd = row % 2 == 1
    at_x, at_y = lax.axis_index("gx"), lax.axis_index("gy")
    last_x, last_y = lax.axis_size("gx") - 1, lax.axis_size("gy") - 1

    def along_third(value):
        total = third[0] * value
        for shift in range(1, SIDE):
            total = total + third[shift] * roll_rows(value, 2 * shift)
        return total

    def ends(up, down):
        total = in_low * roll_lanes(roll_rows(up, 2), 1) - own_low * up
        return total + in_high * roll_lanes(roll_rows(down, -2), -1) - own_high * down

    def start(value, old):
        return value if old is None else F32(0.5) * (value + old)

    for side in range(2):
        there = at_x > 0 if side == 0 else at_x < last_x
        m = [[now.x(k, side, i, b) for i in range(3)] for b in range(SIDE)]
        e = [cross(ghost_at(ghost_speed, side * SIDE + b), m[b]) for b in range(SIDE)]
        for b in (1, 2):
            own = m[b][0]
            total = weighted(table[b], [e[q][2] for q in range(SIDE)]) - along_third(e[b][1])
            total = total + ends(own + e[b][1], own - e[b][1])
            total = total + F32(jump) * (state[k, 0, (SIDE - 1) * side, b] - own)
            old = None if before is None else before.x(k, side, 0, b)
            inner_x[k, side, b - 1] = pick(there, start(own, old) + total, zero)
    m = [[now.y(k, i, a) for i in range(3)] for a in range(SIDE)]
    e = [cross(ghost_at(ghost_speed, 2 * SIDE + a), m[a]) for a in range(SIDE)]
    for a in (1, 2):
        own = m[a][1]
        total = along_third(e[a][0]) - weighted(table[a], [e[q][2] for q in range(SIDE)])
        total = total + ends(own - e[a][0], own + e[a][0])
        mine = jnp.where(odd, state[k, 1, a, SIDE - 1], state[k, 1, a, 0])
        total = total + F32(jump) * (mine - own)
        old = None if before is None else before.y(k, 1, a)
        value = start(own, old) + total
        low = pick(at_y > 0, value, zero)
        high = pick(at_y < last_y, value, zero)
        inner_y[k, a - 1] = jnp.where(odd, high, low)


ROWS = 9


def pack_kernel(velocity, out):
    wide = velocity.shape[1]
    pairs = velocity.shape[2] // 2
    lane = lax.broadcasted_iota(jnp.int32, (pairs, 64), 1)
    upper = lane % 16 >= 12

    def both(q, x):
        return [velocity[q, x, pl.ds(j, pairs, stride=2), :] for j in range(2)]

    def store(x, q, value):
        out[pl.ds(x * pairs * ROWS + q, pairs, stride=ROWS), :] = value

    for x in range(wide):
        for q in range(6):
            store(x, q, jnp.concatenate(both(q, x), axis=1))
        for q in range(3):
            even, odd = both(q, x)
            even_low, odd_low = both(q, (x - 1) % wide)
            even_high, odd_high = both(q, (x + 1) % wide)
            y_part = jnp.where(upper, pltpu.roll(odd, 1, 0), pltpu.roll(even, pairs - 1, 0))
            store(
                x,
                6 + q,
                jnp.concatenate(
                    [
                        y_part,
                        even_high[:, :16],
                        odd_high[:, :16],
                        odd_low[:, 48:],
                        even_low[:, 48:],
                    ],
                    axis=1,
                ),
            )


def faces_kernel(state, *faces):
    px, py = parities()

    def step(k, carry):
        send_faces(k, FULL, state, None, px, py, *faces)
        return carry

    lax.fori_loop(0, KRYLOV, step, 0)


def unpack_kernel(arrived, first, second, ghosts):
    for q in range(ROWS):
        block = arrived[pl.ds(q, LANES, stride=ROWS), :].T
        if q < 6:
            into = first if q < 3 else second
            into[q % 3, pl.ds(0, 64, stride=2), :] = block[:64]
            into[q % 3, pl.ds(1, 64, stride=2), :] = block[64:]
        else:
            i = q - 6
            ghosts[i, pl.ds(0, 16, stride=2), :] = block[112:]
            ghosts[i, pl.ds(1, 16, stride=2), :] = block[96:112]
            ghosts[i, pl.ds(32, 16, stride=2), :] = block[64:80]
            ghosts[i, pl.ds(33, 16, stride=2), :] = block[80:96]
            for a in range(SIDE):
                ghosts[i, pl.ds(64 + a * 8, 4, stride=2), :] = block[a * 16 + 12 : a * 16 + 16]
                ghosts[i, pl.ds(65 + a * 8, 4, stride=2), :] = block[a * 16 : a * 16 + 4]


def first_volume_kernel(state, speed, pre, elec):
    def base(k, a, b):
        return [state[k, i, a, b] for i in range(3)]

    def step(k, carry):
        volume(k, state, base, speed, elec, pre, STEP_SIZE)
        return carry

    lax.fori_loop(0, KRYLOV, step, 0)


def second_volume_kernel(state, start, speed, pre, elec):
    def base(k, a, b):
        return [F32(0.5) * (state[k, i, a, b] + start[k, i, a, b]) for i in range(3)]

    def step(k, carry):
        volume(k, state, base, speed, elec, pre, 0.5 * STEP_SIZE)
        return carry

    lax.fori_loop(0, KRYLOV, step, 0)


def inside_kernel(coef, forms, *refs):
    px, py = parities()
    state, ghost_speed, *refs, inner_x, inner_y = refs
    stages = []
    for form in forms:
        faces, refs = refs[:4], refs[4:]
        inner = None
        if form.short:
            inner, refs = refs[:2], refs[2:]
        stages.append(Arrived(form, faces, inner, px, py))
    now = stages[0]
    before = stages[1] if len(stages) > 1 else None

    def step(k, carry):
        inside(k, state, now, before, ghost_speed, inner_x, inner_y, coef)
        return carry

    lax.fori_loop(0, KRYLOV, step, 0, unroll=True)


def finish_kernel(coef, form, has_ghosts, next_form, next_speed, *refs):
    px, py = parities()
    pre, *refs = refs
    faces, refs = refs[:4], refs[4:]
    inner = ghosts = speed = None
    if form.short:
        inner, refs = refs[:2], refs[2:]
    if has_ghosts:
        ghosts, *refs = refs
    if next_speed:
        speed, *refs = refs
    out, *leaving = refs
    arrived = Arrived(form, faces, inner, px, py)

    def step(k, carry):
        receive_faces(k, pre, out, ghosts, arrived, coef)
        if next_form is not None:
            send_faces(k, next_form, out, speed, px, py, *leaving)
        return carry

    lax.fori_loop(0, KRYLOV, step, 0, unroll=True)


STATE = (KRYLOV, 3, SIDE, SIDE, 8, LANES)
INNER = [(KRYLOV, 2, 2, 8, LANES), (KRYLOV, 2, 8, LANES)]
SPEED = (3, 128, LANES)
GHOSTS = (3, 96, LANES)


def call(kernel, shapes, flops, *operands, scratch=()):
    whole = pl.BlockSpec(memory_space=pltpu.VMEM)
    return pl.pallas_call(
        kernel,
        out_shape=[jax.ShapeDtypeStruct(shape, F32) for shape in shapes],
        in_specs=[whole] * len(operands),
        out_specs=[whole] * len(shapes),
        scratch_shapes=[pltpu.VMEM(shape, F32) for shape in scratch],
        compiler_params=pltpu.CompilerParams(vmem_limit_bytes=VMEM_LIMIT),
        cost_estimate=pl.CostEstimate(
            flops=flops, bytes_accessed=2 * 1024 * 1024, transcendentals=0
        ),
    )(*operands)


WAITS = (("y_even", 15 * 10**8), ("x_odd", 10**10))


def exchange(faces, waits=WAITS):
    received = []
    for index, face in enumerate(faces):
        axis = "gx" if ORDER[index][0] == "x" else "gy"
        count = lax.axis_size(axis)
        if ORDER[index][2:] == "even":
            pairs = [(i, i ^ 1) for i in range(count)]
        else:
            pairs = [(i, ((i - 1) ^ 1) + 1) for i in range(1, count - 1)]
        received.append(lax.ppermute(face, axis, pairs))
    return in_order(received, waits)


def pass_kernel(arrived, *refs):
    refs[-1][...] = arrived[...]


def in_order(received, waits):
    whole = pl.BlockSpec(memory_space=pltpu.VMEM)
    before = ()
    for name, flops in waits:
        index = ORDER.index(name)
        array = received[index]
        received[index] = pl.pallas_call(
            pass_kernel,
            out_shape=jax.ShapeDtypeStruct(array.shape, F32),
            in_specs=[whole] + [pl.BlockSpec(memory_space=pl.ANY)] * len(before),
            out_specs=whole,
            compiler_params=pltpu.CompilerParams(vmem_limit_bytes=VMEM_LIMIT),
            cost_estimate=pl.CostEstimate(
                flops=flops, bytes_accessed=flops // 100, transcendentals=0
            ),
        )(array, *before)
        before = (received[index],)
    return received


def shards(fields, velocity):
    phases, comps, nodes, slab, wide_x, wide_y = velocity.shape
    devices = lax.axis_size("gx") * lax.axis_size("gy")
    state = fields.reshape(STATE)
    layers = jnp.transpose(velocity, (0, 1, 3, 4, 5, 2))
    layers = layers.reshape(phases * comps, wide_x, wide_y, nodes)
    (packed,) = call(pack_kernel, [(devices * ROWS, LANES)], 10**6, layers)
    packed = packed.reshape(devices, ROWS * LANES)
    moved = lax.all_to_all(packed, ("gx", "gy"), split_axis=0, concat_axis=0, tiled=True)
    moved = moved.reshape(devices * ROWS, LANES)
    arrived = exchange(call(faces_kernel, FULL.shapes(), 10**6, state), ())
    *speeds, ghosts = call(unpack_kernel, [SPEED, SPEED, GHOSTS], 10**6, moved)
    elec = [(3, SIDE, SIDE, 8, LANES)]

    def finish(coef, form, ghosts, next_form, speed, pre, *arrived):
        def kernel(*refs):
            finish_kernel(
                coef, form, ghosts is not None, next_form, speed is not None, *refs
            )

        extra = [array for array in (ghosts, speed) if array is not None]
        shapes = [STATE] if next_form is None else [STATE, *next_form.shapes()]
        return call(kernel, shapes, 10**6, pre, *arrived, *extra)

    def inner(coef, forms, state, *arrived):
        def kernel(*refs):
            inside_kernel(coef, forms, *refs)

        return call(kernel, INNER, 10**7, state, ghosts, *arrived)

    whole, half = STEP_SIZE, 0.5 * STEP_SIZE
    (pre,) = call(first_volume_kernel, [STATE], 10**7, state, speeds[0], scratch=elec)
    middle, *leaving = finish(whole, FULL, ghosts, SHORT, None, pre, *arrived)
    one = list(arrived)
    two = exchange(leaving)
    two += inner(whole, [FULL], state, *one)
    (pre,) = call(second_volume_kernel, [STATE], 10**7, middle, state, speeds[0], scratch=elec)
    state, *leaving = finish(half, SHORT, ghosts, SHORT, speeds[1], pre, *two)
    three = exchange(leaving)
    three += inner(half, [SHORT, FULL], middle, *two, *one)
    (pre,) = call(first_volume_kernel, [STATE], 10**7, state, speeds[1], scratch=elec)
    middle, *leaving = finish(whole, SHORT, None, FULL, speeds[1], pre, *three)
    four = exchange(leaving)
    (pre,) = call(second_volume_kernel, [STATE], 10**7, middle, state, speeds[1], scratch=elec)
    (state,) = finish(half, FULL, None, None, None, pre, *four)
    return state.reshape(fields.shape)


def solution(mesh):
    return jax.shard_map(
        shards,
        mesh=mesh,
        in_specs=(
            P(None, None, None, "gx", "gy", None),
            P(None, None, None, ("gx", "gy"), None, None),
        ),
        out_specs=P(None, None, None, "gx", "gy", None),
        check_vma=False,
    )
```

```python
import jax
import jax.numpy as jnp
import numpy as np
from jax import lax
from jax.experimental import pallas as pl
from jax.experimental.pallas import tpu as pltpu
from jax.sharding import PartitionSpec as P

STEP_SIZE = 0.025
FLUX_COEF = 3.0
KRYLOV = 4
SIDE = 4
LANES = 128
F32 = jnp.float32
VMEM_LIMIT = 24 * 1024 * 1024


def derivative_table():
    points = np.array([-1.0, -1.0 / np.sqrt(5.0), 1.0 / np.sqrt(5.0), 1.0])
    weights_bary = np.ones(4)
    for first in range(4):
        for second in range(4):
            if first != second:
                weights_bary[first] = weights_bary[first] / (points[first] - points[second])
    table = np.zeros((4, 4))
    for first in range(4):
        for second in range(4):
            if first != second:
                table[first, second] = (
                    weights_bary[second] / weights_bary[first] / (points[first] - points[second])
                )
        table[first, first] = -np.sum(table[first])
    return table.astype(np.float32).astype(np.float64)


TABLE = derivative_table()


def rows():
    return lax.broadcasted_iota(jnp.int32, (8, LANES), 0)


def lanes():
    return lax.broadcasted_iota(jnp.int32, (8, LANES), 1)


def roll_rows(value, shift):
    return pltpu.roll(value, shift % 8, 0)


def roll_lanes(value, shift):
    return pltpu.roll(value, shift % LANES, 1)


def cross(u, b):
    return [
        u[1] * b[2] - u[2] * b[1],
        u[2] * b[0] - u[0] * b[2],
        u[0] * b[1] - u[1] * b[0],
    ]


def plus(direction, b, e):
    if direction == 0:
        return [b[0], b[1] - e[2], b[2] + e[1]]
    if direction == 1:
        return [b[0] + e[2], b[1], b[2] - e[0]]
    return [b[0] - e[1], b[1] + e[0], b[2]]


def minus(direction, b, e):
    if direction == 0:
        return [b[0], b[1] + e[2], b[2] - e[1]]
    if direction == 1:
        return [b[0] - e[2], b[1], b[2] + e[0]]
    return [b[0] + e[1], b[1] - e[0], b[2]]


def speed_at(speed, a, b):
    start = (a * SIDE + b) * 8
    return [speed[i, start : start + 8, :] for i in range(3)]


def third_table(coef):
    node = rows() // 2
    parts = []
    for shift in range(SIDE):
        part = jnp.zeros((8, LANES), F32)
        for p in range(SIDE):
            part = jnp.where(node == p, F32(coef * TABLE[p, (p - shift) % SIDE]), part)
        parts.append(part)
    return parts


def weighted(row, terms):
    total = None
    for q in range(SIDE):
        if row[q] != 0.0:
            part = F32(row[q]) * terms[q]
            total = part if total is None else total + part
    return total


class Weights:
    def __init__(self, coef):
        row, lane = rows(), lanes()
        self.table = coef * TABLE
        self.third = third_table(coef)
        self.jump = F32(FLUX_COEF * coef)
        zero = jnp.zeros((8, LANES), F32)
        self.low = row < 4
        low, high = row < 2, row >= 6
        self.own = jnp.where(low | high, self.jump, zero)
        far = (low & (lane > 0)) | (high & (lane < LANES - 1))
        self.other = jnp.where(far, self.jump, zero)
        self.odd = row % 2 == 1
        self.mid_low = jnp.where(self.odd, self.jump, zero)
        self.mid_high = jnp.where(self.odd, zero, self.jump)

    def along_third(self, value):
        total = self.third[0] * value
        for shift in range(1, SIDE):
            total = total + self.third[shift] * roll_rows(value, 2 * shift)
        return total

    def ends(self, up, down):
        below, above = roll_lanes(roll_rows(up, 2), 1), roll_lanes(roll_rows(down, -2), -1)
        own = up if up is down else jnp.where(self.low, up, down)
        return self.other * jnp.where(self.low, below, above) - self.own * own


def volume(k, state, base, speed, elec, out, weights):
    table, jump = weights.table, weights.jump
    mid_low, mid_high = weights.mid_low, weights.mid_high
    along_third = weights.along_third

    for a in range(SIDE):
        for b in range(SIDE):
            field = [state[k, i, a, b] for i in range(3)]
            parts = cross(speed_at(speed, a, b), field)
            for i in range(3):
                elec[i, a, b] = parts[i]
    for a in range(SIDE):
        for b in range(SIDE):
            e = [elec[i, a, b] for i in range(3)]
            m = [state[k, i, a, b] for i in range(3)]
            total = [
                weighted(table[b], [elec[2, a, q] for q in range(SIDE)]) - along_third(e[1]),
                along_third(e[0]) - weighted(table[a], [elec[2, q, b] for q in range(SIDE)]),
                weighted(table[a], [elec[1, q, b] for q in range(SIDE)])
                - weighted(table[b], [elec[0, a, q] for q in range(SIDE)]),
            ]
            up, down = minus(2, m, e), plus(2, m, e)
            for i in range(3):
                total[i] = total[i] + weights.ends(up[i], down[i])
            if a == 0:
                own = minus(0, m, e)
                total = [t - jump * o for t, o in zip(total, own)]
            if a == SIDE - 1:
                own = plus(0, m, e)
                total = [t - jump * o for t, o in zip(total, own)]
            if b == 0:
                own = minus(1, m, e)
                far_b = [state[k, i, a, SIDE - 1] for i in range(3)]
                far_e = [elec[i, a, SIDE - 1] for i in range(3)]
                far = minus(1, far_b, far_e)
                total = [
                    t - jump * o + mid_low * roll_rows(f, 1)
                    for t, o, f in zip(total, own, far)
                ]
            if b == SIDE - 1:
                own = plus(1, m, e)
                far_b = [state[k, i, a, 0] for i in range(3)]
                far_e = [elec[i, a, 0] for i in range(3)]
                far = plus(1, far_b, far_e)
                total = [
                    t - jump * o + mid_high * roll_rows(f, -1)
                    for t, o, f in zip(total, own, far)
                ]
            start = base(k, a, b)
            for i in range(3):
                out[k, i, a, b] = start[i] + total[i]


def parities():
    return lax.axis_index("gx") % 2 == 1, lax.axis_index("gy") % 2 == 1


def pick(condition, yes, no):
    return jnp.where(condition, yes, no)


def pack_rows(first, second, keep_odd):
    odd = rows() % 2 == 1
    if keep_odd:
        return jnp.where(odd, second, roll_rows(first, -1))
    return jnp.where(odd, roll_rows(second, 1), first)


class Form:
    def __init__(self, short):
        self.short = short
        self.x_count, self.y_count = (10, 5) if short else (12, 6)

    def shapes(self):
        x = (KRYLOV, self.x_count, 8, LANES)
        y = (KRYLOV, self.y_count, 8, LANES)
        return [y if name[0] == "y" else x for name in ORDER]

    def x_slot(self, i, b):
        if not self.short:
            return i * SIDE + b
        if i > 0:
            return (i - 1) * SIDE + b
        return {0: 8, SIDE - 1: 9}.get(b)

    def y_slots(self):
        pairs = [(i, 2 * half, 2 * half + 1) for i in range(3) for half in range(2)]
        if self.short:
            pairs = [p for p in pairs if p[0] != 1] + [(1, 0, SIDE - 1)]
        return pairs


ORDER = ("y_even", "x_odd", "y_odd", "x_even")
FULL, SHORT = Form(False), Form(True)


def send_faces(k, form, state, speed, px, py, y_even, x_odd, y_odd, x_even):
    def traces(direction, sign, a, b):
        m = [state[k, i, a, b] for i in range(3)]
        if speed is None:
            return m
        e = cross(speed_at(speed, a, b), m)
        return plus(direction, m, e) if sign > 0 else minus(direction, m, e)

    for b in range(SIDE):
        high = traces(0, -1, SIDE - 1, b)
        low = traces(0, 1, 0, b)
        for i in range(3):
            slot = form.x_slot(i, b)
            if slot is not None:
                x_even[k, slot] = pick(px, low[i], high[i])
                x_odd[k, slot] = pick(px, high[i], low[i])
    high = [traces(1, -1, a, SIDE - 1) for a in range(SIDE)]
    low = [traces(1, 1, a, 0) for a in range(SIDE)]
    for slot, (i, first, second) in enumerate(form.y_slots()):
        up = pack_rows(high[first][i], high[second][i], True)
        down = pack_rows(low[first][i], low[second][i], False)
        y_even[k, slot] = pick(py, down, up)
        y_odd[k, slot] = pick(py, up, down)


class Arrived:
    def __init__(self, form, faces, inner, px, py):
        self.form, self.inner, self.px, self.py = form, inner, px, py
        self.y_even, self.x_odd, self.y_odd, self.x_even = faces

    def x(self, k, side, i, b):
        slot = self.form.x_slot(i, b)
        if slot is None:
            return self.inner[0][k, side, b - 1]
        even, odd = self.x_even[k, slot], self.x_odd[k, slot]
        return pick(self.px, even, odd) if side == 0 else pick(self.px, odd, even)

    def y(self, k, i, a):
        odd_row = rows() % 2 == 1
        for slot, (comp, first, second) in enumerate(self.form.y_slots()):
            if comp == i and a in (first, second):
                even, odd = self.y_even[k, slot], self.y_odd[k, slot]
                low, high = pick(self.py, even, odd), pick(self.py, odd, even)
                if a == first:
                    return jnp.where(odd_row, roll_rows(high, 1), low)
                return jnp.where(odd_row, high, roll_rows(low, -1))
        return self.inner[1][k, a - 1]


def ghost_at(ghost_speed, place):
    return [ghost_speed[i, place * 8 : place * 8 + 8, :] for i in range(3)]


def receive_faces(k, pre, out, ghost_speed, arrived, coef):
    jump = FLUX_COEF * coef
    odd = rows() % 2 == 1
    zero = jnp.zeros((8, LANES), F32)
    mask_low = jnp.where(odd, zero, F32(jump))
    mask_high = jnp.where(odd, F32(jump), zero)
    turn = jnp.where(odd, F32(1.0), F32(-1.0))
    for b in range(SIDE):
        low = [arrived.x(k, 0, i, b) for i in range(3)]
        high = [arrived.x(k, 1, i, b) for i in range(3)]
        if ghost_speed is not None:
            low = minus(0, low, cross(ghost_at(ghost_speed, b), low))
            high = plus(0, high, cross(ghost_at(ghost_speed, SIDE + b), high))
        for i in range(3):
            out[k, i, 0, b] = pre[k, i, 0, b] + F32(jump) * low[i]
            out[k, i, SIDE - 1, b] = pre[k, i, SIDE - 1, b] + F32(jump) * high[i]
    for a in (1, 2):
        for b in range(SIDE):
            for i in range(3):
                out[k, i, a, b] = pre[k, i, a, b]
    for a in range(SIDE):
        both = [arrived.y(k, i, a) for i in range(3)]
        if ghost_speed is not None:
            e = cross(ghost_at(ghost_speed, 2 * SIDE + a), both)
            both = [both[0] + turn * e[2], both[1], both[2] - turn * e[0]]
        for i in range(3):
            out[k, i, a, 0] = out[k, i, a, 0] + mask_low * both[i]
            out[k, i, a, SIDE - 1] = out[k, i, a, SIDE - 1] + mask_high * both[i]


def inside(k, state, now, before, ghost_speed, inner_x, inner_y, weights):
    table, jump, odd = weights.table, weights.jump, weights.odd
    along_third, ends = weights.along_third, weights.ends
    zero = jnp.zeros((8, LANES), F32)
    at_x, at_y = lax.axis_index("gx"), lax.axis_index("gy")
    last_x, last_y = lax.axis_size("gx") - 1, lax.axis_size("gy") - 1

    def start(value, old):
        return value if old is None else F32(0.5) * (value + old)

    for side in range(2):
        there = at_x > 0 if side == 0 else at_x < last_x
        m = [[now.x(k, side, i, b) for i in range(3)] for b in range(SIDE)]
        e = [cross(ghost_at(ghost_speed, side * SIDE + b), m[b]) for b in range(SIDE)]
        for b in (1, 2):
            own = m[b][0]
            total = weighted(table[b], [e[q][2] for q in range(SIDE)]) - along_third(e[b][1])
            total = total + ends(own + e[b][1], own - e[b][1])
            total = total + jump * (state[k, 0, (SIDE - 1) * side, b] - own)
            old = None if before is None else before.x(k, side, 0, b)
            inner_x[k, side, b - 1] = pick(there, start(own, old) + total, zero)
    m = [[now.y(k, i, a) for i in range(3)] for a in range(SIDE)]
    e = [cross(ghost_at(ghost_speed, 2 * SIDE + a), m[a]) for a in range(SIDE)]
    for a in (1, 2):
        own = m[a][1]
        total = along_third(e[a][0]) - weighted(table[a], [e[q][2] for q in range(SIDE)])
        total = total + ends(own - e[a][0], own + e[a][0])
        mine = jnp.where(odd, state[k, 1, a, SIDE - 1], state[k, 1, a, 0])
        total = total + jump * (mine - own)
        old = None if before is None else before.y(k, 1, a)
        value = start(own, old) + total
        low = pick(at_y > 0, value, zero)
        high = pick(at_y < last_y, value, zero)
        inner_y[k, a - 1] = jnp.where(odd, high, low)


ROWS = 9


def pack_kernel(velocity, out):
    wide = velocity.shape[1]
    pairs = velocity.shape[2] // 2
    lane = lax.broadcasted_iota(jnp.int32, (pairs, 64), 1)
    upper = lane % 16 >= 12

    def both(q, x):
        return [velocity[q, x, pl.ds(j, pairs, stride=2), :] for j in range(2)]

    def store(x, q, value):
        out[pl.ds(x * pairs * ROWS + q, pairs, stride=ROWS), :] = value

    for x in range(wide):
        for q in range(6):
            store(x, q, jnp.concatenate(both(q, x), axis=1))
        for q in range(3):
            even, odd = both(q, x)
            even_low, odd_low = both(q, (x - 1) % wide)
            even_high, odd_high = both(q, (x + 1) % wide)
            y_part = jnp.where(upper, pltpu.roll(odd, 1, 0), pltpu.roll(even, pairs - 1, 0))
            store(
                x,
                6 + q,
                jnp.concatenate(
                    [
                        y_part,
                        even_high[:, :16],
                        odd_high[:, :16],
                        odd_low[:, 48:],
                        even_low[:, 48:],
                    ],
                    axis=1,
                ),
            )


def faces_kernel(state, *faces):
    px, py = parities()

    def step(k, carry):
        send_faces(k, FULL, state, None, px, py, *faces)
        return carry

    lax.fori_loop(0, KRYLOV, step, 0)


def unpack_kernel(arrived, first, second, ghosts):
    for q in range(ROWS):
        block = arrived[pl.ds(q, LANES, stride=ROWS), :].T
        if q < 6:
            into = first if q < 3 else second
            into[q % 3, pl.ds(0, 64, stride=2), :] = block[:64]
            into[q % 3, pl.ds(1, 64, stride=2), :] = block[64:]
        else:
            i = q - 6
            ghosts[i, pl.ds(0, 16, stride=2), :] = block[112:]
            ghosts[i, pl.ds(1, 16, stride=2), :] = block[96:112]
            ghosts[i, pl.ds(32, 16, stride=2), :] = block[64:80]
            ghosts[i, pl.ds(33, 16, stride=2), :] = block[80:96]
            for a in range(SIDE):
                ghosts[i, pl.ds(64 + a * 8, 4, stride=2), :] = block[a * 16 + 12 : a * 16 + 16]
                ghosts[i, pl.ds(65 + a * 8, 4, stride=2), :] = block[a * 16 : a * 16 + 4]


def first_volume_kernel(state, speed, pre, elec):
    weights = Weights(STEP_SIZE)

    def base(k, a, b):
        return [state[k, i, a, b] for i in range(3)]

    def step(k, carry):
        volume(k, state, base, speed, elec, pre, weights)
        return carry

    lax.fori_loop(0, KRYLOV, step, 0, unroll=True)


def second_volume_kernel(state, start, speed, pre, elec):
    weights = Weights(0.5 * STEP_SIZE)

    def base(k, a, b):
        return [F32(0.5) * (state[k, i, a, b] + start[k, i, a, b]) for i in range(3)]

    def step(k, carry):
        volume(k, state, base, speed, elec, pre, weights)
        return carry

    lax.fori_loop(0, KRYLOV, step, 0, unroll=True)


def inside_kernel(coef, forms, *refs):
    px, py = parities()
    state, ghost_speed, *refs, inner_x, inner_y = refs
    stages = []
    for form in forms:
        faces, refs = refs[:4], refs[4:]
        inner = None
        if form.short:
            inner, refs = refs[:2], refs[2:]
        stages.append(Arrived(form, faces, inner, px, py))
    now = stages[0]
    before = stages[1] if len(stages) > 1 else None
    weights = Weights(coef)

    def step(k, carry):
        inside(k, state, now, before, ghost_speed, inner_x, inner_y, weights)
        return carry

    lax.fori_loop(0, KRYLOV, step, 0, unroll=True)


def finish_kernel(coef, form, has_ghosts, next_form, next_speed, *refs):
    px, py = parities()
    pre, *refs = refs
    faces, refs = refs[:4], refs[4:]
    inner = ghosts = speed = None
    if form.short:
        inner, refs = refs[:2], refs[2:]
    if has_ghosts:
        ghosts, *refs = refs
    if next_speed:
        speed, *refs = refs
    out, *leaving = refs
    arrived = Arrived(form, faces, inner, px, py)

    def step(k, carry):
        receive_faces(k, pre, out, ghosts, arrived, coef)
        if next_form is not None:
            send_faces(k, next_form, out, speed, px, py, *leaving)
        return carry

    lax.fori_loop(0, KRYLOV, step, 0, unroll=True)


def last_kernel(coef, pre, *refs):
    *faces, result, out, written = refs
    px, py = parities()
    arrived = Arrived(FULL, faces, None, px, py)

    def copy(k):
        return pltpu.make_async_copy(out.at[k], result.at[k], written.at[k])

    for k in range(KRYLOV):
        receive_faces(k, pre, out, None, arrived, coef)
        copy(k).start()
    for k in range(KRYLOV):
        copy(k).wait()


STATE = (KRYLOV, 3, SIDE, SIDE, 8, LANES)
INNER = [(KRYLOV, 2, 2, 8, LANES), (KRYLOV, 2, 8, LANES)]
SPEED = (3, 128, LANES)
GHOSTS = (3, 96, LANES)


def call(kernel, shapes, flops, *operands, scratch=()):
    whole = pl.BlockSpec(memory_space=pltpu.VMEM)
    return pl.pallas_call(
        kernel,
        out_shape=[jax.ShapeDtypeStruct(shape, F32) for shape in shapes],
        in_specs=[whole] * len(operands),
        out_specs=[whole] * len(shapes),
        scratch_shapes=[pltpu.VMEM(shape, F32) for shape in scratch],
        compiler_params=pltpu.CompilerParams(vmem_limit_bytes=VMEM_LIMIT),
        cost_estimate=pl.CostEstimate(
            flops=flops, bytes_accessed=2 * 1024 * 1024, transcendentals=0
        ),
    )(*operands)


WAITS = (("y_even", 15 * 10**8), ("x_odd", 10**10))


def exchange(faces, waits=WAITS):
    received = []
    for index, face in enumerate(faces):
        axis = "gx" if ORDER[index][0] == "x" else "gy"
        count = lax.axis_size(axis)
        if ORDER[index][2:] == "even":
            pairs = [(i, i ^ 1) for i in range(count)]
        else:
            pairs = [(i, ((i - 1) ^ 1) + 1) for i in range(1, count - 1)]
        received.append(lax.ppermute(face, axis, pairs))
    return in_order(received, waits)


def pass_kernel(arrived, *refs):
    refs[-1][...] = arrived[...]


def in_order(received, waits):
    whole = pl.BlockSpec(memory_space=pltpu.VMEM)
    before = ()
    for name, flops in waits:
        index = ORDER.index(name)
        array = received[index]
        received[index] = pl.pallas_call(
            pass_kernel,
            out_shape=jax.ShapeDtypeStruct(array.shape, F32),
            in_specs=[whole] + [pl.BlockSpec(memory_space=pl.ANY)] * len(before),
            out_specs=whole,
            compiler_params=pltpu.CompilerParams(vmem_limit_bytes=VMEM_LIMIT),
            cost_estimate=pl.CostEstimate(
                flops=flops, bytes_accessed=flops // 100, transcendentals=0
            ),
        )(array, *before)
        before = (received[index],)
    return received


def shards(fields, velocity):
    phases, comps, nodes, slab, wide_x, wide_y = velocity.shape
    devices = lax.axis_size("gx") * lax.axis_size("gy")
    state = fields.reshape(STATE)
    layers = jnp.transpose(velocity, (0, 1, 3, 4, 5, 2))
    layers = layers.reshape(phases * comps, wide_x, wide_y, nodes)
    (packed,) = call(pack_kernel, [(devices * ROWS, LANES)], 10**6, layers)
    packed = packed.reshape(devices, ROWS * LANES)
    moved = lax.all_to_all(packed, ("gx", "gy"), split_axis=0, concat_axis=0, tiled=True)
    moved = moved.reshape(devices * ROWS, LANES)
    arrived = exchange(call(faces_kernel, FULL.shapes(), 10**6, state), ())
    *speeds, ghosts = call(unpack_kernel, [SPEED, SPEED, GHOSTS], 10**6, moved)
    elec = [(3, SIDE, SIDE, 8, LANES)]

    def finish(coef, form, ghosts, next_form, speed, pre, *arrived):
        def kernel(*refs):
            finish_kernel(
                coef, form, ghosts is not None, next_form, speed is not None, *refs
            )

        extra = [array for array in (ghosts, speed) if array is not None]
        shapes = [STATE] if next_form is None else [STATE, *next_form.shapes()]
        return call(kernel, shapes, 10**6, pre, *arrived, *extra)

    def inner(coef, forms, state, *arrived):
        def kernel(*refs):
            inside_kernel(coef, forms, *refs)

        return call(kernel, INNER, 10**7, state, ghosts, *arrived)

    whole, half = STEP_SIZE, 0.5 * STEP_SIZE
    (pre,) = call(first_volume_kernel, [STATE], 10**7, state, speeds[0], scratch=elec)
    middle, *leaving = finish(whole, FULL, ghosts, SHORT, None, pre, *arrived)
    one = list(arrived)
    two = exchange(leaving)
    two += inner(whole, [FULL], state, *one)
    (pre,) = call(second_volume_kernel, [STATE], 10**7, middle, state, speeds[0], scratch=elec)
    state, *leaving = finish(half, SHORT, ghosts, SHORT, speeds[1], pre, *two)
    three = exchange(leaving)
    three += inner(half, [SHORT, FULL], middle, *two, *one)
    (pre,) = call(first_volume_kernel, [STATE], 10**7, state, speeds[1], scratch=elec)
    middle, *leaving = finish(whole, SHORT, None, FULL, speeds[1], pre, *three)
    four = exchange(leaving)
    (pre,) = call(second_volume_kernel, [STATE], 10**7, middle, state, speeds[1], scratch=elec)

    def last(*refs):
        last_kernel(half, *refs)

    state = pl.pallas_call(
        last,
        out_shape=jax.ShapeDtypeStruct(STATE, F32),
        in_specs=[pl.BlockSpec(memory_space=pltpu.VMEM)] * 5,
        out_specs=pl.BlockSpec(memory_space=pltpu.HBM),
        scratch_shapes=[pltpu.VMEM(STATE, F32), pltpu.SemaphoreType.DMA((KRYLOV,))],
        compiler_params=pltpu.CompilerParams(vmem_limit_bytes=VMEM_LIMIT),
        cost_estimate=pl.CostEstimate(flops=10**6, bytes_accessed=2 * 10**6, transcendentals=0),
    )(pre, *four)
    return state.reshape(fields.shape)


def solution(mesh):
    return jax.shard_map(
        shards,
        mesh=mesh,
        in_specs=(
            P(None, None, None, "gx", "gy", None),
            P(None, None, None, ("gx", "gy"), None, None),
        ),
        out_specs=P(None, None, None, "gx", "gy", None),
        check_vma=False,
    )
```
